512 devices in a mesh: dp: 16 (over z_hi, x), fsdp: 32 (over y, z_lo, core).
Axes of the slice: x: 4, y: 8, z: 8 (z_hi: 4, z_lo: 2; z = z_hi * 2 + z_lo), core: 2. Of those that a mesh axis runs over, the one named last changes fastest.
Arguments:
- tokens: bfloat16 [32768, 8192], P('fsdp', 'dp'), may hold values from -6 to 6
- tangent: bfloat16 [32768, 16384], P('fsdp', 'dp'), may hold values from -0.15625 to 0.15625
- projector: bfloat16 [8192, 512], P('dp'), may hold values from -0.0625 to 0.0625
- first_moment: float32 [16384, 512], P(('dp', 'fsdp')), may hold values from -6 to 6
- second_moment: float32 [16384, 512], P(('dp', 'fsdp')), may hold values from 0.3 to 3
Outputs:
- update: bfloat16 [16384, 8192], P(('dp', 'fsdp'))
- new_first: float32 [16384, 512], P(('dp', 'fsdp'))
- new_second: float32 [16384, 512], P(('dp', 'fsdp'))
The draws below stay inside these ranges and needn't reach their ends.
All inputs are finite; a program needn't handle non-finite values.
Results may differ from the reference program's by a relative error of at most 0.0049.
Values may be sent and summed in bfloat16 or wider, within the bound.
No kernel may reach another device: no remote copies, remote signals or barrier semaphores. Data moves between devices by JAX's collectives and lax.ppermute only.
A program may use at most 64 MiB of HBM per device.

```python
import math
import jax
import jax.numpy as jnp

D = 8192
FF = 16384
R = 512
STEP = 10
TOKENS = 32768


def spiked(array, stream_key, source, target, parts, factor):
    owner, partner = [(jnp.arange(array.shape[axis_at]) // (array.shape[axis_at] // parts)).reshape([-1 if axis == axis_at else 1 for axis in range(array.ndim)]) for axis_at in (source, target)]
    chosen = jax.random.permutation(stream_key, parts)[partner]
    strong = (owner == chosen) | (owner == (partner + parts // 2) % parts)
    return jnp.where(strong, factor * array, array)


def shard_levels(own_key, extent, split, least, high):
    def one(position, parts):
        draws = jax.random.uniform(jax.random.fold_in(jax.random.fold_in(own_key, 6), position), (parts,), jnp.float32, least / len(split), high / len(split))
        return jnp.repeat(jnp.exp(draws), extent[position] // parts).reshape((-1,) + (1,) * (len(extent) - position - 1))

    gain = one(*split[0])
    for cut in split[1:]:
        gain = gain * one(*cut)
    return gain


def centred(key, dims, spread, bound, shards=(), dtype=jnp.bfloat16):
    array = spread * jax.random.normal(key, dims, jnp.float32)
    if shards:
        array = array * shard_levels(key, dims, shards, -0.22, 0.18)
    return jnp.clip(array, -bound, bound).astype(dtype)


def noise_with(key, dims, scale, reach, split, heavy, kind=jnp.bfloat16):
    entries = scale * jax.random.normal(key, dims, jnp.float32)
    if split:
        entries = entries * shard_levels(key, dims, split, -0.22, 0.18)
    return jnp.clip(spiked(entries, jax.random.fold_in(key, 3), *heavy), -reach, reach).astype(kind)


def setup_inputs(seed: int = 0) -> dict:
    keys = jax.random.split(jax.random.key(seed), 6)
    tokens = centred(keys[0], (TOKENS, D), 1.0, 6.0, ((0, 32), (1, 16)))
    tangent = noise_with(keys[1], (TOKENS, FF), (TOKENS ** -0.5), 0.15625, ((0, 32), (1, 16)), (0, 1, 32, 2.75))
    projector = centred(keys[2], (D, R), D ** -0.5, 0.0625, ((0, 16),))
    first_moment = centred(keys[3], (FF, R), 1.0, 6.0, ((0, 512),), jnp.float32)
    second_moment = jnp.clip(jnp.exp(math.log(3.0) - 2.3025851 * jax.random.uniform(keys[4], (FF, R), jnp.float32) ** shard_levels(keys[4], (FF, R), ((0, 512),), -0.2, 0.2)), 0.3, 3.0)
    return dict(tokens=tokens, tangent=tangent, projector=projector, first_moment=first_moment, second_moment=second_moment)


def reference(tokens, tangent, projector, first_moment, second_moment):
    reduced = jnp.dot(tokens, projector, preferred_element_type=jnp.float32).astype(jnp.bfloat16)
    gradient = jnp.dot(tangent.T, reduced, preferred_element_type=jnp.float32)
    new_first = 0.9 * first_moment + 0.1 * gradient
    new_second = 0.999 * second_moment + 0.001 * gradient * gradient
    first_fix = 1.0 - 0.9 ** STEP
    second_fix = 1.0 - 0.999 ** STEP
    direction = (new_first / first_fix / (jnp.sqrt(new_second / second_fix) + 1e-08)).astype(jnp.bfloat16)
    update = jnp.dot(direction, projector.T, preferred_element_type=jnp.float32).astype(jnp.bfloat16)
    return (update, new_first, new_second)
```

```python
import jax
import jax.numpy as jnp
from jax import lax
from jax.sharding import Mesh, PartitionSpec as P

STEP = 10
F32 = jnp.float32
BF16 = jnp.bfloat16


def swap(parts, axis):
    return lax.all_to_all(parts, axis, 0, 0)


def add(parts):
    return jnp.sum(parts.astype(F32), axis=0)


def spread(block, axis, n):
    return swap(jnp.broadcast_to(block[None], (n,) + block.shape), axis)


def local(tokens, tangent, projector, first_moment, second_moment):
    r = projector.shape[1]
    wide = lax.all_gather(projector, "zh", axis=0, tiled=True)
    part = jnp.dot(tokens, projector, preferred_element_type=F32).astype(BF16)
    part = add(swap(part.reshape(4, -1, r), "x")).astype(BF16)
    part = add(swap(part.reshape(4, -1, r), "zh")).astype(BF16)
    reduced = spread(part, "zh", 4).reshape(-1, r)
    reduced = spread(reduced, "x", 4).reshape(-1, r)
    grad = lax.dot_general(
        tangent, reduced, (((0,), (0,)), ((), ())), preferred_element_type=F32
    ).astype(BF16)
    grad = grad.reshape(8, 2, 2, -1, r).transpose(2, 1, 0, 3, 4)
    grad = add(swap(grad, "c")).astype(BF16)
    grad = add(swap(grad, "zl")).astype(BF16)
    gradient = add(swap(grad, "y"))

    new_first = 0.9 * first_moment + 0.1 * gradient
    new_second = 0.999 * second_moment + 0.001 * gradient * gradient
    first_fix = 1.0 - 0.9**STEP
    second_fix = 1.0 - 0.999**STEP
    direction = (new_first / first_fix / (jnp.sqrt(new_second / second_fix) + 1e-08)).astype(BF16)
    rows = direction.shape[0]
    directions = spread(direction, "x", 4).reshape(-1, r)
    out = lax.dot_general(
        directions, wide, (((1,), (1,)), ((), ())), preferred_element_type=F32
    ).astype(BF16)
    out = swap(out.reshape(4, rows, -1), "x")
    out = out.reshape(4, rows, 4, -1).transpose(1, 2, 0, 3).reshape(rows, -1)
    return (out, new_first, new_second)


def solution(mesh):
    fine = Mesh(mesh.devices.reshape(4, 4, 8, 2, 2), ("zh", "x", "y", "zl", "c"))
    dp, fsdp = ("zh", "x"), ("y", "zl", "c")
    rows = P(dp + fsdp, None)
    return jax.shard_map(
        local,
        mesh=fine,
        in_specs=(P(fsdp, dp), P(fsdp, dp), P(dp, None), rows, rows),
        out_specs=(rows, rows, rows),
        check_vma=False,
    )
```

```python
import jax
import jax.numpy as jnp
from jax import lax
from jax.sharding import Mesh, PartitionSpec as P

STEP = 10
F32 = jnp.float32
BF16 = jnp.bfloat16


def swap(parts, axis):
    return lax.all_to_all(parts, axis, 0, 0)


def add(parts):
    total = parts[0].astype(F32)
    for i in range(1, parts.shape[0]):
        total = total + parts[i].astype(F32)
    return total


def spread(block, axis, n):
    return swap(jnp.broadcast_to(block[None], (n,) + block.shape), axis)


def local(tokens, tangent, projector, first_moment, second_moment):
    r = projector.shape[1]
    core = lax.axis_index("c")
    half = r // 2
    mine = lax.all_gather(
        lax.dynamic_slice_in_dim(projector, core * half, half, 1), ("zh", "x"), axis=0, tiled=True
    )
    part = jnp.dot(tokens, projector, preferred_element_type=F32).astype(BF16)
    part = add(swap(part.reshape(4, -1, r), "x")).astype(BF16)
    part = add(swap(part.reshape(4, -1, r), "zh")).astype(BF16)
    reduced = spread(part, "zh", 4).reshape(-1, r)
    reduced = spread(reduced, "x", 4).reshape(-1, r)
    grad = lax.dot_general(
        tangent, reduced, (((0,), (0,)), ((), ())), preferred_element_type=F32
    ).astype(BF16)
    mine, grad = lax.optimization_barrier((mine, grad))
    other = lax.ppermute(mine, "c", [(0, 1), (1, 0)])
    grad = grad.reshape(8, 2, 2, -1, r).transpose(2, 1, 0, 3, 4)
    grad = add(swap(grad.reshape(2, -1, r), "c")).astype(BF16)
    grad = add(swap(grad.reshape(2, -1, r), "zl")).astype(BF16)
    gradient = add(swap(grad.reshape(8, -1, r), "y"))

    new_first = 0.9 * first_moment + 0.1 * gradient
    new_second = 0.999 * second_moment + 0.001 * gradient * gradient
    first_fix = 1.0 - 0.9**STEP
    second_fix = 1.0 - 0.999**STEP
    direction = (new_first / first_fix / (jnp.sqrt(new_second / second_fix) + 1e-08)).astype(BF16)
    contract = (((1,), (1,)), ((), ()))
    out = lax.dot_general(
        lax.dynamic_slice_in_dim(direction, core * half, half, 1),
        mine,
        contract,
        preferred_element_type=F32,
    )
    out = out + lax.dot_general(
        lax.dynamic_slice_in_dim(direction, (1 - core) * half, half, 1),
        other,
        contract,
        preferred_element_type=F32,
    )
    out = out.astype(BF16)
    return (out, new_first, new_second)


def solution(mesh):
    fine = Mesh(mesh.devices.reshape(4, 4, 8, 2, 2), ("zh", "x", "y", "zl", "c"))
    dp, fsdp = ("zh", "x"), ("y", "zl", "c")
    rows = P(dp + fsdp, None)
    return jax.shard_map(
        local,
        mesh=fine,
        in_specs=(P(fsdp, dp), P(fsdp, dp), P(dp, None), rows, rows),
        out_specs=(rows, rows, rows),
        check_vma=False,
    )
```

```python
import jax
import jax.numpy as jnp
from jax import lax
from jax.experimental import pallas as pl
from jax.experimental.pallas import tpu as pltpu
from jax.sharding import Mesh, PartitionSpec as P

STEP = 10
F32 = jnp.float32
BF16 = jnp.bfloat16


def swap(parts, axis):
    return lax.all_to_all(parts, axis, 0, 0)


def add(parts):
    total = parts[0].astype(F32)
    for i in range(1, parts.shape[0]):
        total = total + parts[i].astype(F32)
    return total


def scattered_sum(part, axis, n):
    return add(swap(part.reshape((n, -1) + part.shape[1:]), axis))


def spread(block, axis, n):
    return swap(jnp.broadcast_to(block[None], (n,) + block.shape), axis)


def turn_kernel(in_ref, out_ref):
    turned = in_ref[...].T
    rows = out_ref.shape[2]
    for i in range(out_ref.shape[1]):
        for c in range(2):
            at = (2 * i + c) * rows
            out_ref[c, i] = turned[at : at + rows]


def turn(tangent):
    tokens, hidden = tangent.shape
    rows = hidden // 32
    step = 128 // (2 * rows)
    out = pl.pallas_call(
        turn_kernel,
        grid=(hidden // 128,),
        in_specs=[pl.BlockSpec((tokens, 128), lambda i: (0, i))],
        out_specs=pl.BlockSpec((2, step, rows, tokens), lambda i: (0, i, 0, 0)),
        out_shape=jax.ShapeDtypeStruct((2, 16, rows, tokens), tangent.dtype),
        cost_estimate=pl.CostEstimate(flops=0, bytes_accessed=4 * tokens * hidden, transcendentals=0),
        compiler_params=pltpu.CompilerParams(vmem_limit_bytes=16 * 2**20),
    )(tangent)
    return out.reshape(hidden, tokens)


def product_kernel(a_ref, b_ref, out_ref):
    step = 256

    @pl.loop(0, a_ref.shape[0] // step)
    def _(i):
        at = pl.ds(pl.multiple_of(i * step, step), step)
        out_ref[at] = jnp.dot(a_ref[at], b_ref[...], preferred_element_type=F32).astype(BF16)


def product(a, b):
    vmem = pl.BlockSpec(memory_space=pltpu.VMEM)
    m, k, n = a.shape[0], a.shape[1], b.shape[1]
    return pl.pallas_call(
        product_kernel,
        in_specs=[vmem, vmem],
        out_specs=vmem,
        out_shape=jax.ShapeDtypeStruct((m, n), BF16),
        cost_estimate=pl.CostEstimate(
            flops=2 * m * k * n, bytes_accessed=2 * (m * k + k * n + m * n), transcendentals=0
        ),
        compiler_params=pltpu.CompilerParams(vmem_limit_bytes=16 * 2**20),
    )(a, b)


def weave_kernel(core_ref, mine_ref, other_ref, out_ref):
    core = core_ref[0]
    for z in range(out_ref.shape[0]):
        for y in range(out_ref.shape[1]):
            out_ref[z, y, core] = mine_ref[y, z]
            out_ref[z, y, 1 - core] = other_ref[y, z]


def weave(core, mine, other):
    y, z, rows, r = mine.shape
    vmem = pl.BlockSpec(memory_space=pltpu.VMEM)
    out = pl.pallas_call(
        weave_kernel,
        in_specs=[pl.BlockSpec(memory_space=pltpu.SMEM), vmem, vmem],
        out_specs=vmem,
        out_shape=jax.ShapeDtypeStruct((z, y, 2, rows, r), mine.dtype),
        cost_estimate=pl.CostEstimate(flops=0, bytes_accessed=8 * mine.size, transcendentals=0),
        compiler_params=pltpu.CompilerParams(vmem_limit_bytes=16 * 2**20),
    )(core.reshape(1), mine, other)
    return out.reshape(-1, r)


def lay_kernel(in_ref, out_ref):
    n = in_ref.shape[0]
    width = in_ref.shape[2] // n
    for z in range(n):
        for x in range(n):
            at = (z * n + x) * width
            out_ref[:, at : at + width] = in_ref[x, :, z * width : (z + 1) * width]


def lay(blocks):
    n, rows, columns = blocks.shape
    vmem = pl.BlockSpec(memory_space=pltpu.VMEM)
    return pl.pallas_call(
        lay_kernel,
        in_specs=[vmem],
        out_specs=vmem,
        out_shape=jax.ShapeDtypeStruct((rows, n * columns), blocks.dtype),
        cost_estimate=pl.CostEstimate(flops=0, bytes_accessed=4 * blocks.size, transcendentals=0),
        compiler_params=pltpu.CompilerParams(vmem_limit_bytes=16 * 2**20),
    )(blocks)


def local(tokens, tangent, projector, first_moment, second_moment):
    r = projector.shape[1]
    core = lax.axis_index("c")
    share = projector.shape[0] // 16
    piece = lax.dynamic_slice_in_dim(projector, (lax.axis_index("y") * 2 + core) * share, share, 0)
    pieces = spread(piece, "zh", 4)
    mine = spread(pieces, "y", 8)
    tt = turn(tangent)
    part = jnp.dot(tokens, projector, preferred_element_type=F32).astype(BF16)
    part = scattered_sum(part, ("zh", "x"), 16).astype(BF16)
    reduced = spread(part, ("zh", "x"), 16).reshape(-1, r)
    grad = product(tt, reduced)
    mine, grad = lax.optimization_barrier((mine, grad))
    other = lax.ppermute(mine, "c", [(0, 1), (1, 0)])
    grad = scattered_sum(grad, "c", 2).astype(BF16)
    gradient = scattered_sum(grad, ("y", "zl"), 16)
    wide = weave(core, mine, other)

    new_first = 0.9 * first_moment + 0.1 * gradient
    new_second = 0.999 * second_moment + 0.001 * gradient * gradient
    first_fix = 1.0 - 0.9**STEP
    second_fix = 1.0 - 0.999**STEP
    direction = (new_first / first_fix / (jnp.sqrt(new_second / second_fix) + 1e-08)).astype(BF16)
    rows = direction.shape[0]
    directions = spread(direction, "x", 4).reshape(-1, r)
    out = lax.dot_general(
        directions, wide, (((1,), (1,)), ((), ())), preferred_element_type=F32
    ).astype(BF16)
    out = lay(swap(out.reshape(4, rows, -1), "x"))
    return (out, new_first, new_second)


def solution(mesh):
    fine = Mesh(mesh.devices.reshape(4, 4, 8, 2, 2), ("zh", "x", "y", "zl", "c"))
    dp, fsdp = ("zh", "x"), ("y", "zl", "c")
    rows = P(dp + fsdp, None)
    return jax.shard_map(
        local,
        mesh=fine,
        in_specs=(P(fsdp, dp), P(fsdp, dp), P(dp, None), rows, rows),
        out_specs=(rows, rows, rows),
        check_vma=False,
    )
```

```python
import jax
import jax.numpy as jnp
from jax import lax
from jax.experimental import pallas as pl
from jax.experimental.pallas import tpu as pltpu
from jax.sharding import Mesh, PartitionSpec as P

STEP = 10
F32 = jnp.float32
BF16 = jnp.bfloat16


def swap(parts, axis):
    return lax.all_to_all(parts, axis, 0, 0)


def add(parts):
    total = parts[0].astype(F32)
    for i in range(1, parts.shape[0]):
        total = total + parts[i].astype(F32)
    return total


def scattered_sum(part, axis, n):
    return add(swap(part.reshape((n, -1) + part.shape[1:]), axis))


def spread(block, axis, n):
    return swap(jnp.broadcast_to(block[None], (n,) + block.shape), axis)


def rotate(block, axis, n):
    return [block] + [
        lax.ppermute(block, axis, [(i, (i + k) % n) for i in range(n)]) for k in range(1, n)
    ]


def turn_kernel(in_ref, out_ref):
    turned = in_ref[...].T
    rows = out_ref.shape[2]
    for i in range(out_ref.shape[1]):
        for c in range(2):
            at = (2 * i + c) * rows
            out_ref[c, i] = turned[at : at + rows]


def turn(tangent):
    tokens, hidden = tangent.shape
    rows = hidden // 32
    step = 128 // (2 * rows)
    out = pl.pallas_call(
        turn_kernel,
        grid=(hidden // 128,),
        in_specs=[pl.BlockSpec((tokens, 128), lambda i: (0, i))],
        out_specs=pl.BlockSpec((2, step, rows, tokens), lambda i: (0, i, 0, 0)),
        out_shape=jax.ShapeDtypeStruct((2, 16, rows, tokens), tangent.dtype),
        cost_estimate=pl.CostEstimate(flops=0, bytes_accessed=4 * tokens * hidden, transcendentals=0),
        compiler_params=pltpu.CompilerParams(vmem_limit_bytes=16 * 2**20),
    )(tangent)
    return out.reshape(hidden, tokens)


def product_kernel(a_ref, b_ref, out_ref):
    step = 256

    @pl.loop(0, a_ref.shape[0] // step)
    def _(i):
        at = pl.ds(pl.multiple_of(i * step, step), step)
        out_ref[at] = jnp.dot(a_ref[at], b_ref[...], preferred_element_type=F32).astype(BF16)


def product(a, b):
    vmem = pl.BlockSpec(memory_space=pltpu.VMEM)
    m, k, n = a.shape[0], a.shape[1], b.shape[1]
    return pl.pallas_call(
        product_kernel,
        in_specs=[vmem, vmem],
        out_specs=vmem,
        out_shape=jax.ShapeDtypeStruct((m, n), BF16),
        cost_estimate=pl.CostEstimate(
            flops=2 * m * k * n, bytes_accessed=2 * (m * k + k * n + m * n), transcendentals=0
        ),
        compiler_params=pltpu.CompilerParams(vmem_limit_bytes=16 * 2**20),
    )(a, b)


def weave_kernel(at_ref, mine_ref, other_ref, out_ref):
    z, y, core = at_ref[0], at_ref[1], at_ref[2]
    for i in range(mine_ref.shape[0]):
        for j in range(mine_ref.shape[1]):
            to_z, to_y = lax.rem(z + 4 - j, 4), lax.rem(y + 8 - i, 8)
            out_ref[to_z, to_y, core] = mine_ref[i, j]
            out_ref[to_z, to_y, 1 - core] = other_ref[i, j]


def weave(at, mine, other):
    y, z, rows, r = mine.shape
    vmem = pl.BlockSpec(memory_space=pltpu.VMEM)
    out = pl.pallas_call(
        weave_kernel,
        in_specs=[pl.BlockSpec(memory_space=pltpu.SMEM), vmem, vmem],
        out_specs=vmem,
        out_shape=jax.ShapeDtypeStruct((z, y, 2, rows, r), mine.dtype),
        cost_estimate=pl.CostEstimate(flops=0, bytes_accessed=8 * mine.size, transcendentals=0),
        compiler_params=pltpu.CompilerParams(vmem_limit_bytes=16 * 2**20),
    )(at, mine, other)
    return out.reshape(-1, r)


def lay_kernel(in_ref, out_ref):
    n = in_ref.shape[0]
    width = in_ref.shape[2] // n
    for z in range(n):
        for x in range(n):
            at = (z * n + x) * width
            out_ref[:, at : at + width] = in_ref[x, :, z * width : (z + 1) * width]


def lay(blocks):
    n, rows, columns = blocks.shape
    vmem = pl.BlockSpec(memory_space=pltpu.VMEM)
    return pl.pallas_call(
        lay_kernel,
        in_specs=[vmem],
        out_specs=vmem,
        out_shape=jax.ShapeDtypeStruct((rows, n * columns), blocks.dtype),
        cost_estimate=pl.CostEstimate(flops=0, bytes_accessed=4 * blocks.size, transcendentals=0),
        compiler_params=pltpu.CompilerParams(vmem_limit_bytes=16 * 2**20),
    )(blocks)


def local(tokens, tangent, projector, first_moment, second_moment):
    r = projector.shape[1]
    z, y, core = lax.axis_index("zh"), lax.axis_index("y"), lax.axis_index("c")
    share = projector.shape[0] // 16
    piece = lax.dynamic_slice_in_dim(projector, (y * 2 + core) * share, share, 0)
    pieces = jnp.stack(rotate(piece, "zh", 4))
    tt = turn(tangent)
    part = jnp.dot(tokens, projector, preferred_element_type=F32).astype(BF16)
    part = scattered_sum(part, ("zh", "x"), 16).astype(BF16)
    pieces, tt, part = lax.optimization_barrier((pieces, tt, part))
    mine = jnp.stack(rotate(pieces, "y", 8))
    reduced = spread(part, ("zh", "x"), 16).reshape(-1, r)
    grad = product(tt, reduced)
    mine, grad = lax.optimization_barrier((mine, grad))
    grad = scattered_sum(grad, "c", 2).astype(BF16)
    other = lax.ppermute(mine, "c", [(0, 1), (1, 0)])
    gradient = scattered_sum(grad, ("y", "zl"), 16)
    wide = weave(jnp.stack([z, y, core]).astype(jnp.int32), mine, other)

    new_first = 0.9 * first_moment + 0.1 * gradient
    new_second = 0.999 * second_moment + 0.001 * gradient * gradient
    first_fix = 1.0 - 0.9**STEP
    second_fix = 1.0 - 0.999**STEP
    direction = (new_first / first_fix / (jnp.sqrt(new_second / second_fix) + 1e-08)).astype(BF16)
    rows = direction.shape[0]
    directions = spread(direction, "x", 4).reshape(-1, r)
    out = lax.dot_general(
        directions, wide, (((1,), (1,)), ((), ())), preferred_element_type=F32
    ).astype(BF16)
    out = lay(swap(out.reshape(4, rows, -1), "x"))
    return (out, new_first, new_second)


def solution(mesh):
    fine = Mesh(mesh.devices.reshape(4, 4, 8, 2, 2), ("zh", "x", "y", "zl", "c"))
    dp, fsdp = ("zh", "x"), ("y", "zl", "c")
    rows = P(dp + fsdp, None)
    return jax.shard_map(
        local,
        mesh=fine,
        in_specs=(P(fsdp, dp), P(fsdp, dp), P(dp, None), rows, rows),
        out_specs=(rows, rows, rows),
        check_vma=False,
    )
```

```python
import jax
import jax.numpy as jnp
from jax import lax
from jax.experimental import pallas as pl
from jax.experimental.pallas import tpu as pltpu
from jax.sharding import Mesh, PartitionSpec as P

STEP = 10
F32 = jnp.float32
BF16 = jnp.bfloat16


def swap(parts, axis):
    return lax.all_to_all(parts, axis, 0, 0)


def add(parts):
    total = parts[0].astype(F32)
    for i in range(1, parts.shape[0]):
        total = total + parts[i].astype(F32)
    return total


def scattered_sum(part, axis, n):
    return add(swap(part.reshape((n, -1) + part.shape[1:]), axis))


def spread(block, axis, n):
    return swap(jnp.broadcast_to(block[None], (n,) + block.shape), axis)


def back(block, axis, n, k):
    return lax.ppermute(block, axis, [(i, (i + k) % n) for i in range(n)])


def turn_kernel(in_ref, out_ref):
    turned = in_ref[...].T
    rows = out_ref.shape[2]
    for i in range(out_ref.shape[1]):
        for c in range(2):
            at = (2 * i + c) * rows
            out_ref[c, i] = turned[at : at + rows]


def turn(tangent):
    tokens, hidden = tangent.shape
    rows = hidden // 32
    step = 128 // (2 * rows)
    out = pl.pallas_call(
        turn_kernel,
        grid=(hidden // 128,),
        in_specs=[pl.BlockSpec((tokens, 128), lambda i: (0, i))],
        out_specs=pl.BlockSpec((2, step, rows, tokens), lambda i: (0, i, 0, 0)),
        out_shape=jax.ShapeDtypeStruct((2, 16, rows, tokens), tangent.dtype),
        cost_estimate=pl.CostEstimate(flops=0, bytes_accessed=4 * tokens * hidden, transcendentals=0),
        compiler_params=pltpu.CompilerParams(vmem_limit_bytes=16 * 2**20),
    )(tangent)
    return out.reshape(hidden, tokens)


def product_kernel(a_ref, b_ref, out_ref):
    step = 256

    @pl.loop(0, a_ref.shape[0] // step)
    def _(i):
        at = pl.ds(pl.multiple_of(i * step, step), step)
        out_ref[at] = jnp.dot(a_ref[at], b_ref[...], preferred_element_type=F32).astype(BF16)


def product(a, b):
    vmem = pl.BlockSpec(memory_space=pltpu.VMEM)
    m, k, n = a.shape[0], a.shape[1], b.shape[1]
    return pl.pallas_call(
        product_kernel,
        in_specs=[vmem, vmem],
        out_specs=vmem,
        out_shape=jax.ShapeDtypeStruct((m, n), BF16),
        cost_estimate=pl.CostEstimate(
            flops=2 * m * k * n, bytes_accessed=2 * (m * k + k * n + m * n), transcendentals=0
        ),
        compiler_params=pltpu.CompilerParams(vmem_limit_bytes=16 * 2**20),
    )(a, b)


def weave_kernel(at_ref, own_ref, mine_ref, other_ref, out_ref):
    z, core = at_ref[0], at_ref[1]
    half = own_ref.shape[0] // 2
    out_ref[z, 0] = own_ref[:half]
    out_ref[z, 1] = own_ref[half:]
    for k in range(mine_ref.shape[0]):
        to = lax.rem(z + 3 - k, 4)
        out_ref[to, core] = mine_ref[k]
        out_ref[to, 1 - core] = other_ref[k]


def weave(at, own, mine, other):
    back_z, rows, r = mine.shape
    vmem = pl.BlockSpec(memory_space=pltpu.VMEM)
    out = pl.pallas_call(
        weave_kernel,
        in_specs=[pl.BlockSpec(memory_space=pltpu.SMEM), vmem, vmem, vmem],
        out_specs=vmem,
        out_shape=jax.ShapeDtypeStruct((back_z + 1, 2, rows, r), mine.dtype),
        cost_estimate=pl.CostEstimate(flops=0, bytes_accessed=8 * mine.size, transcendentals=0),
        compiler_params=pltpu.CompilerParams(vmem_limit_bytes=16 * 2**20),
    )(at, own, mine, other)
    return out.reshape(-1, r)


def lay_kernel(in_ref, out_ref):
    n = in_ref.shape[0]
    width = in_ref.shape[2] // n
    for z in range(n):
        for x in range(n):
            at = (z * n + x) * width
            out_ref[:, at : at + width] = in_ref[x, :, z * width : (z + 1) * width]


def lay(blocks):
    n, rows, columns = blocks.shape
    vmem = pl.BlockSpec(memory_space=pltpu.VMEM)
    return pl.pallas_call(
        lay_kernel,
        in_specs=[vmem],
        out_specs=vmem,
        out_shape=jax.ShapeDtypeStruct((rows, n * columns), blocks.dtype),
        cost_estimate=pl.CostEstimate(flops=0, bytes_accessed=4 * blocks.size, transcendentals=0),
        compiler_params=pltpu.CompilerParams(vmem_limit_bytes=16 * 2**20),
    )(blocks)


def local(tokens, tangent, projector, first_moment, second_moment):
    r = projector.shape[1]
    z, core = lax.axis_index("zh"), lax.axis_index("c")
    tt = turn(tangent)
    half = projector.shape[0] // 2
    share = lax.dynamic_slice_in_dim(projector, core * half, half, 0)
    one, three = back(share, "zh", 4, 1), back(share, "zh", 4, 3)
    part = jnp.dot(tokens, projector, preferred_element_type=F32).astype(BF16)
    part = scattered_sum(part, "x", 4).astype(BF16)
    one, three, tt, part = lax.optimization_barrier((one, three, tt, part))
    part = scattered_sum(part, "zh", 4).astype(BF16)
    part = spread(part, "zh", 4).reshape(-1, r)
    share, part = lax.optimization_barrier((share, part))
    two = back(share, "zh", 4, 2)
    reduced = spread(part, "x", 4).reshape(-1, r)
    two, reduced = lax.optimization_barrier((two, reduced))
    grad = product(tt, reduced)
    grad = scattered_sum(grad, "c", 2).astype(BF16)
    one, two, three, grad = lax.optimization_barrier((one, two, three, grad))
    mine = jnp.stack([one, two, three])
    other = lax.ppermute(mine, "c", [(0, 1), (1, 0)])
    gradient = scattered_sum(grad, ("y", "zl"), 16)
    wide = weave(jnp.stack([z, core]).astype(jnp.int32), projector, mine, other)

    new_first = 0.9 * first_moment + 0.1 * gradient
    new_second = 0.999 * second_moment + 0.001 * gradient * gradient
    first_fix = 1.0 - 0.9**STEP
    second_fix = 1.0 - 0.999**STEP
    direction = (new_first / first_fix / (jnp.sqrt(new_second / second_fix) + 1e-08)).astype(BF16)
    rows = direction.shape[0]
    directions = spread(direction, "x", 4).reshape(-1, r)
    out = lax.dot_general(
        directions, wide, (((1,), (1,)), ((), ())), preferred_element_type=F32
    ).astype(BF16)
    out = lay(swap(out.reshape(4, rows, -1), "x"))
    return (out, new_first, new_second)


def solution(mesh):
    fine = Mesh(mesh.devices.reshape(4, 4, 8, 2, 2), ("zh", "x", "y", "zl", "c"))
    dp, fsdp = ("zh", "x"), ("y", "zl", "c")
    rows = P(dp + fsdp, None)
    return jax.shard_map(
        local,
        mesh=fine,
        in_specs=(P(fsdp, dp), P(fsdp, dp), P(dp, None), rows, rows),
        out_specs=(rows, rows, rows),
        check_vma=False,
    )
```

```python
import jax
import jax.numpy as jnp
from jax import lax
from jax.experimental import pallas as pl
from jax.experimental.pallas import tpu as pltpu
from jax.sharding import Mesh, PartitionSpec as P

STEP = 10
F32 = jnp.float32
BF16 = jnp.bfloat16


def swap(parts, axis):
    return lax.all_to_all(parts, axis, 0, 0)


def add(parts):
    total = parts[0].astype(F32)
    for i in range(1, parts.shape[0]):
        total = total + parts[i].astype(F32)
    return total


def scattered_sum(part, axis, n):
    return add(swap(part.reshape((n, -1) + part.shape[1:]), axis))


def spread(block, axis, n):
    return swap(jnp.broadcast_to(block[None], (n,) + block.shape), axis)


def back(block, axis, n, k):
    return lax.ppermute(block, axis, [(i, (i + k) % n) for i in range(n)])


def turn_kernel(in_ref, out_ref):
    turned = in_ref[...].T
    rows = out_ref.shape[2]
    for i in range(out_ref.shape[1]):
        for c in range(2):
            at = (2 * i + c) * rows
            out_ref[c, i] = turned[at : at + rows]


def turn(tangent):
    tokens, hidden = tangent.shape
    rows = hidden // 32
    step = 128 // (2 * rows)
    out = pl.pallas_call(
        turn_kernel,
        grid=(hidden // 128,),
        in_specs=[pl.BlockSpec((tokens, 128), lambda i: (0, i))],
        out_specs=pl.BlockSpec((2, step, rows, tokens), lambda i: (0, i, 0, 0)),
        out_shape=jax.ShapeDtypeStruct((2, 16, rows, tokens), tangent.dtype),
        cost_estimate=pl.CostEstimate(flops=0, bytes_accessed=4 * tokens * hidden, transcendentals=0),
        compiler_params=pltpu.CompilerParams(vmem_limit_bytes=16 * 2**20),
    )(tangent)
    return out.reshape(hidden, tokens)


def product_kernel(a_ref, b_ref, out_ref):
    step = 256

    @pl.loop(0, a_ref.shape[0] // step)
    def _(i):
        at = pl.ds(pl.multiple_of(i * step, step), step)
        out_ref[at] = jnp.dot(a_ref[at], b_ref[...], preferred_element_type=F32).astype(BF16)


def product(a, b):
    vmem = pl.BlockSpec(memory_space=pltpu.VMEM)
    m, k, n = a.shape[0], a.shape[1], b.shape[1]
    return pl.pallas_call(
        product_kernel,
        in_specs=[vmem, vmem],
        out_specs=vmem,
        out_shape=jax.ShapeDtypeStruct((m, n), BF16),
        cost_estimate=pl.CostEstimate(
            flops=2 * m * k * n, bytes_accessed=2 * (m * k + k * n + m * n), transcendentals=0
        ),
        compiler_params=pltpu.CompilerParams(vmem_limit_bytes=16 * 2**20),
    )(a, b)


def weave_kernel(at_ref, own_ref, mine_ref, other_ref, out_ref):
    z, core, odd = at_ref[0], at_ref[1], at_ref[2]
    rows = own_ref.shape[0] // 4
    for i in range(4):
        out_ref[z, i // 2, i % 2] = own_ref[i * rows : (i + 1) * rows]
    for k in range(mine_ref.shape[1]):
        to = lax.rem(z + 3 - k, 4)
        out_ref[to, core, odd] = mine_ref[0, k]
        out_ref[to, core, 1 - odd] = mine_ref[1, k]
        out_ref[to, 1 - core, odd] = other_ref[0, k]
        out_ref[to, 1 - core, 1 - odd] = other_ref[1, k]


def weave(at, own, mine, other):
    _, back_z, rows, r = mine.shape
    vmem = pl.BlockSpec(memory_space=pltpu.VMEM)
    out = pl.pallas_call(
        weave_kernel,
        in_specs=[pl.BlockSpec(memory_space=pltpu.SMEM), vmem, vmem, vmem],
        out_specs=vmem,
        out_shape=jax.ShapeDtypeStruct((back_z + 1, 2, 2, rows, r), mine.dtype),
        cost_estimate=pl.CostEstimate(flops=0, bytes_accessed=8 * mine.size, transcendentals=0),
        compiler_params=pltpu.CompilerParams(vmem_limit_bytes=16 * 2**20),
    )(at, own, mine, other)
    return out.reshape(-1, r)


def lay_kernel(in_ref, out_ref):
    n = in_ref.shape[0]
    width = in_ref.shape[2] // n
    for z in range(n):
        for x in range(n):
            at = (z * n + x) * width
            out_ref[:, at : at + width] = in_ref[x, :, z * width : (z + 1) * width]


def lay(blocks):
    n, rows, columns = blocks.shape
    vmem = pl.BlockSpec(memory_space=pltpu.VMEM)
    return pl.pallas_call(
        lay_kernel,
        in_specs=[vmem],
        out_specs=vmem,
        out_shape=jax.ShapeDtypeStruct((rows, n * columns), blocks.dtype),
        cost_estimate=pl.CostEstimate(flops=0, bytes_accessed=4 * blocks.size, transcendentals=0),
        compiler_params=pltpu.CompilerParams(vmem_limit_bytes=16 * 2**20),
    )(blocks)


def local(tokens, tangent, projector, first_moment, second_moment):
    r = projector.shape[1]
    z, core, odd = lax.axis_index("zh"), lax.axis_index("c"), lax.axis_index("y") % 2
    tt = turn(tangent)
    rows = projector.shape[0] // 4
    share = lax.dynamic_slice_in_dim(projector, (core * 2 + odd) * rows, rows, 0)
    shares = [back(share, "zh", 4, k) for k in (1, 2, 3)]
    part = jnp.dot(tokens, projector, preferred_element_type=F32).astype(BF16)
    part = scattered_sum(part, "x", 4).astype(BF16)
    *shares, tt, part = lax.optimization_barrier((*shares, tt, part))
    part = scattered_sum(part, "zh", 4).astype(BF16)
    shares = jnp.stack(shares)
    neighbour = lax.ppermute(shares, "y", [(i, i ^ 1) for i in range(8)])
    reduced = spread(part, ("x", "zh"), 16).reshape(-1, r)
    neighbour, reduced = lax.optimization_barrier((neighbour, reduced))
    grad = product(tt, reduced)
    grad = scattered_sum(grad, "c", 2).astype(BF16)
    shares, neighbour, grad = lax.optimization_barrier((shares, neighbour, grad))
    mine = jnp.stack([shares, neighbour])
    other = lax.ppermute(mine, "c", [(0, 1), (1, 0)])
    gradient = scattered_sum(grad, ("y", "zl"), 16)
    wide = weave(jnp.stack([z, core, odd]).astype(jnp.int32), projector, mine, other)

    new_first = 0.9 * first_moment + 0.1 * gradient
    new_second = 0.999 * second_moment + 0.001 * gradient * gradient
    first_fix = 1.0 - 0.9**STEP
    second_fix = 1.0 - 0.999**STEP
    direction = (new_first / first_fix / (jnp.sqrt(new_second / second_fix) + 1e-08)).astype(BF16)
    rows = direction.shape[0]
    directions = spread(direction, "x", 4).reshape(-1, r)
    out = lax.dot_general(
        directions, wide, (((1,), (1,)), ((), ())), preferred_element_type=F32
    ).astype(BF16)
    out = lay(swap(out.reshape(4, rows, -1), "x"))
    return (out, new_first, new_second)


def solution(mesh):
    fine = Mesh(mesh.devices.reshape(4, 4, 8, 2, 2), ("zh", "x", "y", "zl", "c"))
    dp, fsdp = ("zh", "x"), ("y", "zl", "c")
    rows = P(dp + fsdp, None)
    return jax.shard_map(
        local,
        mesh=fine,
        in_specs=(P(fsdp, dp), P(fsdp, dp), P(dp, None), rows, rows),
        out_specs=(rows, rows, rows),
        check_vma=False,
    )
```

```python
import jax
import jax.numpy as jnp
from jax import lax
from jax.experimental import pallas as pl
from jax.experimental.pallas import tpu as pltpu
from jax.sharding import Mesh, PartitionSpec as P

STEP = 10
F32 = jnp.float32
BF16 = jnp.bfloat16


def swap(parts, axis):
    return lax.all_to_all(parts, axis, 0, 0)


def add(parts):
    total = parts[0].astype(F32)
    for i in range(1, parts.shape[0]):
        total = total + parts[i].astype(F32)
    return total


def scattered_sum(part, axis, n):
    return add(swap(part.reshape((n, -1) + part.shape[1:]), axis))


def spread(block, axis, n):
    return swap(jnp.broadcast_to(block[None], (n,) + block.shape), axis)


def turn_kernel(in_ref, out_ref):
    turned = in_ref[...].T
    rows = out_ref.shape[2]
    for i in range(out_ref.shape[1]):
        for c in range(2):
            at = (2 * i + c) * rows
            out_ref[c, i] = turned[at : at + rows]


def turn(tangent):
    tokens, hidden = tangent.shape
    rows = hidden // 32
    step = 128 // (2 * rows)
    out = pl.pallas_call(
        turn_kernel,
        grid=(hidden // 128,),
        in_specs=[pl.BlockSpec((tokens, 128), lambda i: (0, i))],
        out_specs=pl.BlockSpec((2, step, rows, tokens), lambda i: (0, i, 0, 0)),
        out_shape=jax.ShapeDtypeStruct((2, 16, rows, tokens), tangent.dtype),
        cost_estimate=pl.CostEstimate(flops=0, bytes_accessed=4 * tokens * hidden, transcendentals=0),
        compiler_params=pltpu.CompilerParams(vmem_limit_bytes=16 * 2**20),
    )(tangent)
    return out.reshape(hidden, tokens)


def product_kernel(a_ref, b_ref, out_ref):
    step = 256

    @pl.loop(0, a_ref.shape[0] // step)
    def _(i):
        at = pl.ds(pl.multiple_of(i * step, step), step)
        out_ref[at] = jnp.dot(a_ref[at], b_ref[...], preferred_element_type=F32).astype(BF16)


def product(a, b):
    vmem = pl.BlockSpec(memory_space=pltpu.VMEM)
    m, k, n = a.shape[0], a.shape[1], b.shape[1]
    return pl.pallas_call(
        product_kernel,
        in_specs=[vmem, vmem],
        out_specs=vmem,
        out_shape=jax.ShapeDtypeStruct((m, n), BF16),
        cost_estimate=pl.CostEstimate(
            flops=2 * m * k * n, bytes_accessed=2 * (m * k + k * n + m * n), transcendentals=0
        ),
        compiler_params=pltpu.CompilerParams(vmem_limit_bytes=16 * 2**20),
    )(a, b)


def lay_kernel(in_ref, out_ref):
    n = in_ref.shape[0]
    width = in_ref.shape[2] // n
    for z in range(n):
        for x in range(n):
            at = (z * n + x) * width
            out_ref[:, at : at + width] = in_ref[x, :, z * width : (z + 1) * width]


def lay(blocks):
    n, rows, columns = blocks.shape
    vmem = pl.BlockSpec(memory_space=pltpu.VMEM)
    return pl.pallas_call(
        lay_kernel,
        in_specs=[vmem],
        out_specs=vmem,
        out_shape=jax.ShapeDtypeStruct((rows, n * columns), blocks.dtype),
        cost_estimate=pl.CostEstimate(flops=0, bytes_accessed=4 * blocks.size, transcendentals=0),
        compiler_params=pltpu.CompilerParams(vmem_limit_bytes=16 * 2**20),
    )(blocks)


def local(tokens, tangent, projector, first_moment, second_moment):
    r = projector.shape[1]
    share = projector.shape[0] // 16
    at = (lax.axis_index("y") * 2 + lax.axis_index("c")) * share
    piece = lax.dynamic_slice_in_dim(projector, at, share, 0)
    wide = lax.all_gather(piece, ("zh", "y", "c"), axis=0, tiled=True)
    tt = turn(tangent)
    part = jnp.dot(tokens, projector, preferred_element_type=F32).astype(BF16)
    part = scattered_sum(part, ("zh", "x"), 16).astype(BF16)
    tt, part = lax.optimization_barrier((tt, part))
    reduced = spread(part, ("zh", "x"), 16).reshape(-1, r)
    grad = product(tt, reduced)
    grad = scattered_sum(grad, "c", 2).astype(BF16)
    gradient = scattered_sum(grad, ("y", "zl"), 16)

    new_first = 0.9 * first_moment + 0.1 * gradient
    new_second = 0.999 * second_moment + 0.001 * gradient * gradient
    first_fix = 1.0 - 0.9**STEP
    second_fix = 1.0 - 0.999**STEP
    direction = (new_first / first_fix / (jnp.sqrt(new_second / second_fix) + 1e-08)).astype(BF16)
    rows = direction.shape[0]
    directions = spread(direction, "x", 4).reshape(-1, r)
    out = lax.dot_general(
        directions, wide, (((1,), (1,)), ((), ())), preferred_element_type=F32
    ).astype(BF16)
    out = lay(swap(out.reshape(4, rows, -1), "x"))
    return (out, new_first, new_second)


def solution(mesh):
    fine = Mesh(mesh.devices.reshape(4, 4, 8, 2, 2), ("zh", "x", "y", "zl", "c"))
    dp, fsdp = ("zh", "x"), ("y", "zl", "c")
    rows = P(dp + fsdp, None)
    return jax.shard_map(
        local,
        mesh=fine,
        in_specs=(P(fsdp, dp), P(fsdp, dp), P(dp, None), rows, rows),
        out_specs=(rows, rows, rows),
        check_vma=False,
    )
```

```python
import jax
import jax.numpy as jnp
from jax import lax
from jax.experimental import pallas as pl
from jax.experimental.pallas import tpu as pltpu
from jax.sharding import Mesh, PartitionSpec as P

STEP = 10
F32 = jnp.float32
BF16 = jnp.bfloat16


def swap(parts, axis):
    return lax.all_to_all(parts, axis, 0, 0)


def add(parts):
    total = parts[0].astype(F32)
    for i in range(1, parts.shape[0]):
        total = total + parts[i].astype(F32)
    return total


def scattered_sum(part, axis, n):
    return add(swap(part.reshape((n, -1) + part.shape[1:]), axis))


def spread(block, axis, n):
    return swap(jnp.broadcast_to(block[None], (n,) + block.shape), axis)


def back(block, axis, n, k):
    return lax.ppermute(block, axis, [(i, (i + k) % n) for i in range(n)])


def turn_kernel(in_ref, out_ref):
    turned = in_ref[...].T
    rows = out_ref.shape[2]
    for i in range(out_ref.shape[1]):
        for c in range(2):
            at = (2 * i + c) * rows
            out_ref[c, i] = turned[at : at + rows]


def turn(tangent):
    tokens, hidden = tangent.shape
    rows = hidden // 32
    step = 128 // (2 * rows)
    out = pl.pallas_call(
        turn_kernel,
        grid=(hidden // 128,),
        in_specs=[pl.BlockSpec((tokens, 128), lambda i: (0, i))],
        out_specs=pl.BlockSpec((2, step, rows, tokens), lambda i: (0, i, 0, 0)),
        out_shape=jax.ShapeDtypeStruct((2, 16, rows, tokens), tangent.dtype),
        cost_estimate=pl.CostEstimate(flops=0, bytes_accessed=4 * tokens * hidden, transcendentals=0),
        compiler_params=pltpu.CompilerParams(vmem_limit_bytes=16 * 2**20),
    )(tangent)
    return out.reshape(hidden, tokens)


def product_kernel(a_ref, b_ref, out_ref):
    step = 256

    @pl.loop(0, a_ref.shape[0] // step)
    def _(i):
        at = pl.ds(pl.multiple_of(i * step, step), step)
        out_ref[at] = jnp.dot(a_ref[at], b_ref[...], preferred_element_type=F32).astype(BF16)


def product(a, b):
    vmem = pl.BlockSpec(memory_space=pltpu.VMEM)
    m, k, n = a.shape[0], a.shape[1], b.shape[1]
    return pl.pallas_call(
        product_kernel,
        in_specs=[vmem, vmem],
        out_specs=vmem,
        out_shape=jax.ShapeDtypeStruct((m, n), BF16),
        cost_estimate=pl.CostEstimate(
            flops=2 * m * k * n, bytes_accessed=2 * (m * k + k * n + m * n), transcendentals=0
        ),
        compiler_params=pltpu.CompilerParams(vmem_limit_bytes=16 * 2**20),
    )(a, b)


def weave_kernel(at_ref, own_ref, mine_ref, other_ref, out_ref):
    z, core = at_ref[0], at_ref[1]
    half = own_ref.shape[0] // 2
    out_ref[z, 0] = own_ref[:half]
    out_ref[z, 1] = own_ref[half:]
    for k in range(mine_ref.shape[0]):
        to = lax.rem(z + 3 - k, 4)
        out_ref[to, core] = mine_ref[k]
        out_ref[to, 1 - core] = other_ref[k]


def weave(at, own, mine, other):
    back_z, rows, r = mine.shape
    vmem = pl.BlockSpec(memory_space=pltpu.VMEM)
    out = pl.pallas_call(
        weave_kernel,
        in_specs=[pl.BlockSpec(memory_space=pltpu.SMEM), vmem, vmem, vmem],
        out_specs=vmem,
        out_shape=jax.ShapeDtypeStruct((back_z + 1, 2, rows, r), mine.dtype),
        cost_estimate=pl.CostEstimate(flops=0, bytes_accessed=8 * mine.size, transcendentals=0),
        compiler_params=pltpu.CompilerParams(vmem_limit_bytes=16 * 2**20),
    )(at, own, mine, other)
    return out.reshape(-1, r)


def lay_kernel(in_ref, out_ref):
    n = in_ref.shape[0]
    width = in_ref.shape[2] // n
    for z in range(n):
        for x in range(n):
            at = (z * n + x) * width
            out_ref[:, at : at + width] = in_ref[x, :, z * width : (z + 1) * width]


def lay(blocks):
    n, rows, columns = blocks.shape
    vmem = pl.BlockSpec(memory_space=pltpu.VMEM)
    return pl.pallas_call(
        lay_kernel,
        in_specs=[vmem],
        out_specs=vmem,
        out_shape=jax.ShapeDtypeStruct((rows, n * columns), blocks.dtype),
        cost_estimate=pl.CostEstimate(flops=0, bytes_accessed=4 * blocks.size, transcendentals=0),
        compiler_params=pltpu.CompilerParams(vmem_limit_bytes=16 * 2**20),
    )(blocks)


def local(tokens, tangent, projector, first_moment, second_moment):
    r = projector.shape[1]
    z, core = lax.axis_index("zh"), lax.axis_index("c")
    tt = turn(tangent)
    part = jnp.dot(tokens, projector, preferred_element_type=F32).astype(BF16)
    part = scattered_sum(part, ("zh", "x"), 16).astype(BF16)
    tt, part = lax.optimization_barrier((tt, part))
    reduced = spread(part, ("zh", "x"), 16).reshape(-1, r)
    grad = product(tt, reduced)
    grad = scattered_sum(grad, "c", 2).astype(BF16)
    half = projector.shape[0] // 2
    share = lax.dynamic_slice_in_dim(projector, core * half, half, 0)
    share, grad = lax.optimization_barrier((share, grad))
    mine = jnp.stack([back(share, "zh", 4, k) for k in (1, 2, 3)])
    gradient = scattered_sum(grad, ("y", "zl"), 16)
    mine, gradient = lax.optimization_barrier((mine, gradient))
    other = lax.ppermute(mine, "c", [(0, 1), (1, 0)])
    wide = weave(jnp.stack([z, core]).astype(jnp.int32), projector, mine, other)

    new_first = 0.9 * first_moment + 0.1 * gradient
    new_second = 0.999 * second_moment + 0.001 * gradient * gradient
    first_fix = 1.0 - 0.9**STEP
    second_fix = 1.0 - 0.999**STEP
    direction = (new_first / first_fix / (jnp.sqrt(new_second / second_fix) + 1e-08)).astype(BF16)
    rows = direction.shape[0]
    directions = spread(direction, "x", 4).reshape(-1, r)
    out = lax.dot_general(
        directions, wide, (((1,), (1,)), ((), ())), preferred_element_type=F32
    ).astype(BF16)
    out = lay(swap(out.reshape(4, rows, -1), "x"))
    return (out, new_first, new_second)


def solution(mesh):
    fine = Mesh(mesh.devices.reshape(4, 4, 8, 2, 2), ("zh", "x", "y", "zl", "c"))
    dp, fsdp = ("zh", "x"), ("y", "zl", "c")
    rows = P(dp + fsdp, None)
    return jax.shard_map(
        local,
        mesh=fine,
        in_specs=(P(fsdp, dp), P(fsdp, dp), P(dp, None), rows, rows),
        out_specs=(rows, rows, rows),
        check_vma=False,
    )
```

```python
import jax
import jax.numpy as jnp
from jax import lax
from jax.experimental import pallas as pl
from jax.experimental.pallas import tpu as pltpu
from jax.sharding import Mesh, PartitionSpec as P

STEP = 10
F32 = jnp.float32
BF16 = jnp.bfloat16


def swap(parts, axis):
    return lax.all_to_all(parts, axis, 0, 0)


def add(parts):
    total = parts[0].astype(F32)
    for i in range(1, parts.shape[0]):
        total = total + parts[i].astype(F32)
    return total


def scattered_sum(part, axis, n):
    return add(swap(part.reshape((n, -1) + part.shape[1:]), axis))


def spread(block, axis, n):
    return swap(jnp.broadcast_to(block[None], (n,) + block.shape), axis)


def turn_kernel(in_ref, out_ref):
    turned = in_ref[...].T
    rows = out_ref.shape[2]
    for i in range(out_ref.shape[1]):
        for c in range(2):
            at = (2 * i + c) * rows
            out_ref[c, i] = turned[at : at + rows]


def turn(tangent):
    tokens, hidden = tangent.shape
    rows = hidden // 32
    step = 128 // (2 * rows)
    out = pl.pallas_call(
        turn_kernel,
        grid=(hidden // 128,),
        in_specs=[pl.BlockSpec((tokens, 128), lambda i: (0, i))],
        out_specs=pl.BlockSpec((2, step, rows, tokens), lambda i: (0, i, 0, 0)),
        out_shape=jax.ShapeDtypeStruct((2, 16, rows, tokens), tangent.dtype),
        cost_estimate=pl.CostEstimate(flops=0, bytes_accessed=4 * tokens * hidden, transcendentals=0),
        compiler_params=pltpu.CompilerParams(vmem_limit_bytes=16 * 2**20),
    )(tangent)
    return out.reshape(hidden, tokens)


def product_kernel(a_ref, b_ref, out_ref):
    step = 256

    @pl.loop(0, a_ref.shape[0] // step)
    def _(i):
        at = pl.ds(pl.multiple_of(i * step, step), step)
        out_ref[at] = jnp.dot(a_ref[at], b_ref[...], preferred_element_type=F32).astype(BF16)


def product(a, b):
    vmem = pl.BlockSpec(memory_space=pltpu.VMEM)
    m, k, n = a.shape[0], a.shape[1], b.shape[1]
    return pl.pallas_call(
        product_kernel,
        in_specs=[vmem, vmem],
        out_specs=vmem,
        out_shape=jax.ShapeDtypeStruct((m, n), BF16),
        cost_estimate=pl.CostEstimate(
            flops=2 * m * k * n, bytes_accessed=2 * (m * k + k * n + m * n), transcendentals=0
        ),
        compiler_params=pltpu.CompilerParams(vmem_limit_bytes=16 * 2**20),
    )(a, b)


def lay_kernel(in_ref, out_ref):
    width = in_ref.shape[2]
    for i in range(in_ref.shape[0]):
        out_ref[:, i * width : (i + 1) * width] = in_ref[i]


def lay(blocks):
    n, rows, columns = blocks.shape
    vmem = pl.BlockSpec(memory_space=pltpu.VMEM)
    return pl.pallas_call(
        lay_kernel,
        in_specs=[vmem],
        out_specs=vmem,
        out_shape=jax.ShapeDtypeStruct((rows, n * columns), blocks.dtype),
        cost_estimate=pl.CostEstimate(flops=0, bytes_accessed=4 * blocks.size, transcendentals=0),
        compiler_params=pltpu.CompilerParams(vmem_limit_bytes=16 * 2**20),
    )(blocks)


def local(tokens, tangent, projector, first_moment, second_moment):
    r = projector.shape[1]
    tt = turn(tangent)
    part = jnp.dot(tokens, projector, preferred_element_type=F32).astype(BF16)
    part = scattered_sum(part, "x", 4).astype(BF16)
    tt, part = lax.optimization_barrier((tt, part))
    part = scattered_sum(part, "zh", 4).astype(BF16)
    part = spread(part, "zh", 4).reshape(-1, r)
    reduced = spread(part, "x", 4).reshape(-1, r)
    grad = product(tt, reduced)
    grad = scattered_sum(grad, "c", 2).astype(BF16)
    gradient = scattered_sum(grad, ("y", "zl"), 16)

    new_first = 0.9 * first_moment + 0.1 * gradient
    new_second = 0.999 * second_moment + 0.001 * gradient * gradient
    first_fix = 1.0 - 0.9**STEP
    second_fix = 1.0 - 0.999**STEP
    direction = (new_first / first_fix / (jnp.sqrt(new_second / second_fix) + 1e-08)).astype(BF16)
    rows = direction.shape[0]
    directions = spread(direction, ("zh", "x"), 16).reshape(-1, r)
    out = lax.dot_general(
        directions, projector, (((1,), (1,)), ((), ())), preferred_element_type=F32
    ).astype(BF16)
    out = lay(swap(out.reshape(16, rows, -1), ("zh", "x")))
    return (out, new_first, new_second)


def solution(mesh):
    fine = Mesh(mesh.devices.reshape(4, 4, 8, 2, 2), ("zh", "x", "y", "zl", "c"))
    dp, fsdp = ("zh", "x"), ("y", "zl", "c")
    rows = P(dp + fsdp, None)
    return jax.shard_map(
        local,
        mesh=fine,
        in_specs=(P(fsdp, dp), P(fsdp, dp), P(dp, None), rows, rows),
        out_specs=(rows, rows, rows),
        check_vma=False,
    )
```

```python
import jax
import jax.numpy as jnp
from jax import lax
from jax.experimental import pallas as pl
from jax.experimental.pallas import tpu as pltpu
from jax.sharding import Mesh, PartitionSpec as P

STEP = 10
F32 = jnp.float32
BF16 = jnp.bfloat16


def swap(parts, axis):
    return lax.all_to_all(parts, axis, 0, 0)


def add(parts):
    total = parts[0].astype(F32)
    for i in range(1, parts.shape[0]):
        total = total + parts[i].astype(F32)
    return total


def scattered_sum(part, axis, n):
    return add(swap(part.reshape((n, -1) + part.shape[1:]), axis))


def spread(block, axis, n):
    return swap(jnp.broadcast_to(block[None], (n,) + block.shape), axis)


def turn_kernel(in_ref, out_ref):
    turned = in_ref[...].T
    rows = out_ref.shape[2]
    for i in range(out_ref.shape[1]):
        for c in range(2):
            at = (2 * i + c) * rows
            out_ref[c, i] = turned[at : at + rows]


def turn(tangent):
    tokens, hidden = tangent.shape
    rows = hidden // 32
    step = 128 // (2 * rows)
    out = pl.pallas_call(
        turn_kernel,
        grid=(hidden // 128,),
        in_specs=[pl.BlockSpec((tokens, 128), lambda i: (0, i))],
        out_specs=pl.BlockSpec((2, step, rows, tokens), lambda i: (0, i, 0, 0)),
        out_shape=jax.ShapeDtypeStruct((2, 16, rows, tokens), tangent.dtype),
        cost_estimate=pl.CostEstimate(flops=0, bytes_accessed=4 * tokens * hidden, transcendentals=0),
        compiler_params=pltpu.CompilerParams(vmem_limit_bytes=16 * 2**20),
    )(tangent)
    return out.reshape(hidden, tokens)


def product_kernel(a_ref, b_ref, out_ref):
    step = 256

    @pl.loop(0, a_ref.shape[0] // step)
    def _(i):
        at = pl.ds(pl.multiple_of(i * step, step), step)
        out_ref[at] = jnp.dot(a_ref[at], b_ref[...], preferred_element_type=F32).astype(BF16)


def cost(m, k, n):
    return pl.CostEstimate(
        flops=2 * m * k * n, bytes_accessed=2 * (m * k + k * n + m * n), transcendentals=0
    )


def product(a, b):
    vmem = pl.BlockSpec(memory_space=pltpu.VMEM)
    m, k, n = a.shape[0], a.shape[1], b.shape[1]
    return pl.pallas_call(
        product_kernel,
        in_specs=[vmem, vmem],
        out_specs=vmem,
        out_shape=jax.ShapeDtypeStruct((m, n), BF16),
        cost_estimate=cost(m, k, n),
        compiler_params=pltpu.CompilerParams(vmem_limit_bytes=16 * 2**20),
    )(a, b)


def rows_kernel(at_ref, dir_ref, own_ref, near_ref, far_ref, out_ref):
    own, core = at_ref[0], at_ref[1]
    width = own_ref.shape[0]
    half = width // 2

    def fill(ref, at):
        out_ref[:, pl.ds(pl.multiple_of(at, half), ref.shape[0])] = lax.dot_general(
            dir_ref[...], ref[...], (((1,), (1,)), ((), ())), preferred_element_type=F32
        ).astype(BF16)

    fill(own_ref, own * width)
    fill(near_ref, (1 - own) * width + core * half)
    fill(far_ref, (1 - own) * width + (1 - core) * half)


def update_rows(at, directions, own, near, far):
    m, k = directions.shape
    n = 2 * own.shape[0]
    vmem = pl.BlockSpec(memory_space=pltpu.VMEM)
    return pl.pallas_call(
        rows_kernel,
        in_specs=[pl.BlockSpec(memory_space=pltpu.SMEM)] + [vmem] * 4,
        out_specs=vmem,
        out_shape=jax.ShapeDtypeStruct((m, n), BF16),
        cost_estimate=cost(m, k, n),
        compiler_params=pltpu.CompilerParams(vmem_limit_bytes=16 * 2**20),
    )(at, directions, own, near, far)


def lay_kernel(in_ref, out_ref):
    n, _, columns = in_ref.shape
    width = columns // 2
    for half in range(2):
        for i in range(n):
            at = (half * n + i) * width
            out_ref[:, at : at + width] = in_ref[i, :, half * width : (half + 1) * width]


def lay(blocks):
    n, rows, columns = blocks.shape
    vmem = pl.BlockSpec(memory_space=pltpu.VMEM)
    return pl.pallas_call(
        lay_kernel,
        in_specs=[vmem],
        out_specs=vmem,
        out_shape=jax.ShapeDtypeStruct((rows, n * columns), blocks.dtype),
        cost_estimate=pl.CostEstimate(flops=0, bytes_accessed=4 * blocks.size, transcendentals=0),
        compiler_params=pltpu.CompilerParams(vmem_limit_bytes=16 * 2**20),
    )(blocks)


def local(tokens, tangent, projector, first_moment, second_moment):
    r = projector.shape[1]
    za, core = lax.axis_index("za"), lax.axis_index("c")
    z = ("za", "zb")
    tt = turn(tangent)
    half = projector.shape[0] // 2
    near = lax.ppermute(
        lax.dynamic_slice_in_dim(projector, core * half, half, 0), "za", [(0, 1), (1, 0)]
    )
    part = jnp.dot(tokens, projector, preferred_element_type=F32).astype(BF16)
    part = scattered_sum(part, "x", 4).astype(BF16)
    near, tt, part = lax.optimization_barrier((near, tt, part))
    part = scattered_sum(part, z, 4).astype(BF16)
    part = spread(part, z, 4).reshape(-1, r)
    near, part = lax.optimization_barrier((near, part))
    far = lax.ppermute(near, "c", [(0, 1), (1, 0)])
    reduced = spread(part, "x", 4).reshape(-1, r)
    far, reduced = lax.optimization_barrier((far, reduced))
    grad = product(tt, reduced)
    grad = scattered_sum(grad, "c", 2).astype(BF16)
    gradient = scattered_sum(grad, ("y", "zl"), 16)

    new_first = 0.9 * first_moment + 0.1 * gradient
    new_second = 0.999 * second_moment + 0.001 * gradient * gradient
    first_fix = 1.0 - 0.9**STEP
    second_fix = 1.0 - 0.999**STEP
    direction = (new_first / first_fix / (jnp.sqrt(new_second / second_fix) + 1e-08)).astype(BF16)
    rows = direction.shape[0]
    directions = spread(direction, ("zb", "x"), 8).reshape(-1, r)
    at = jnp.stack([za, core]).astype(jnp.int32)
    out = update_rows(at, directions, projector, near, far)
    out = lay(swap(out.reshape(8, rows, -1), ("zb", "x")))
    return (out, new_first, new_second)


def solution(mesh):
    fine = Mesh(mesh.devices.reshape(2, 2, 4, 8, 2, 2), ("za", "zb", "x", "y", "zl", "c"))
    dp, fsdp = ("za", "zb", "x"), ("y", "zl", "c")
    rows = P(dp + fsdp, None)
    return jax.shard_map(
        local,
        mesh=fine,
        in_specs=(P(fsdp, dp), P(fsdp, dp), P(dp, None), rows, rows),
        out_specs=(rows, rows, rows),
        check_vma=False,
    )
```

```python
import jax
import jax.numpy as jnp
from jax import lax
from jax.experimental import pallas as pl
from jax.experimental.pallas import tpu as pltpu
from jax.sharding import Mesh, PartitionSpec as P

STEP = 10
F32 = jnp.float32
BF16 = jnp.bfloat16


def swap(parts, axis):
    return lax.all_to_all(parts, axis, 0, 0)


def add(parts):
    total = parts[0].astype(F32)
    for i in range(1, parts.shape[0]):
        total = total + parts[i].astype(F32)
    return total


def scattered_sum(part, axis, n):
    return add(swap(part.reshape((n, -1) + part.shape[1:]), axis))


def spread(block, axis, n):
    return swap(jnp.broadcast_to(block[None], (n,) + block.shape), axis)


def back(block, axis, n, k):
    return lax.ppermute(block, axis, [(i, (i + k) % n) for i in range(n)])


def turn_kernel(in_ref, out_ref):
    turned = in_ref[...].T
    rows = out_ref.shape[2]
    for i in range(out_ref.shape[1]):
        for c in range(2):
            at = (2 * i + c) * rows
            out_ref[c, i] = turned[at : at + rows]


def turn(tangent):
    tokens, hidden = tangent.shape
    rows = hidden // 32
    step = 128 // (2 * rows)
    out = pl.pallas_call(
        turn_kernel,
        grid=(hidden // 128,),
        in_specs=[pl.BlockSpec((tokens, 128), lambda i: (0, i))],
        out_specs=pl.BlockSpec((2, step, rows, tokens), lambda i: (0, i, 0, 0)),
        out_shape=jax.ShapeDtypeStruct((2, 16, rows, tokens), tangent.dtype),
        cost_estimate=pl.CostEstimate(flops=0, bytes_accessed=4 * tokens * hidden, transcendentals=0),
        compiler_params=pltpu.CompilerParams(vmem_limit_bytes=16 * 2**20),
    )(tangent)
    return out.reshape(hidden, tokens)


def product_kernel(a_ref, b_ref, out_ref):
    step = 256

    @pl.loop(0, a_ref.shape[0] // step)
    def _(i):
        at = pl.ds(pl.multiple_of(i * step, step), step)
        out_ref[at] = jnp.dot(a_ref[at], b_ref[...], preferred_element_type=F32).astype(BF16)


def cost(m, k, n):
    return pl.CostEstimate(
        flops=2 * m * k * n, bytes_accessed=2 * (m * k + k * n + m * n), transcendentals=0
    )


def product(a, b):
    vmem = pl.BlockSpec(memory_space=pltpu.VMEM)
    m, k, n = a.shape[0], a.shape[1], b.shape[1]
    return pl.pallas_call(
        product_kernel,
        in_specs=[vmem, vmem],
        out_specs=vmem,
        out_shape=jax.ShapeDtypeStruct((m, n), BF16),
        cost_estimate=cost(m, k, n),
        compiler_params=pltpu.CompilerParams(vmem_limit_bytes=16 * 2**20),
    )(a, b)


def rows_kernel(at_ref, dir_ref, own_ref, mine_ref, other_ref, out_ref):
    z, core = at_ref[0], at_ref[1]
    width = own_ref.shape[0]
    half = width // 2

    def fill(rows, at):
        out_ref[:, pl.ds(pl.multiple_of(at, half), rows.shape[0])] = lax.dot_general(
            dir_ref[...], rows, (((1,), (1,)), ((), ())), preferred_element_type=F32
        ).astype(BF16)

    fill(own_ref[...], z * width)
    for k in range(3):
        at = lax.rem(z + 3 - k, 4) * width
        fill(mine_ref[k], at + core * half)
        fill(other_ref[k], at + (1 - core) * half)


def update_rows(at, directions, own, mine, other):
    m, k = directions.shape
    n = 4 * own.shape[0]
    vmem = pl.BlockSpec(memory_space=pltpu.VMEM)
    return pl.pallas_call(
        rows_kernel,
        in_specs=[pl.BlockSpec(memory_space=pltpu.SMEM)] + [vmem] * 4,
        out_specs=vmem,
        out_shape=jax.ShapeDtypeStruct((m, n), BF16),
        cost_estimate=cost(m, k, n),
        compiler_params=pltpu.CompilerParams(vmem_limit_bytes=16 * 2**20),
    )(at, directions, own, mine, other)


def lay_kernel(in_ref, out_ref):
    n = in_ref.shape[0]
    width = in_ref.shape[2] // n
    for z in range(n):
        for x in range(n):
            at = (z * n + x) * width
            out_ref[:, at : at + width] = in_ref[x, :, z * width : (z + 1) * width]


def lay(blocks):
    n, rows, columns = blocks.shape
    vmem = pl.BlockSpec(memory_space=pltpu.VMEM)
    return pl.pallas_call(
        lay_kernel,
        in_specs=[vmem],
        out_specs=vmem,
        out_shape=jax.ShapeDtypeStruct((rows, n * columns), blocks.dtype),
        cost_estimate=pl.CostEstimate(flops=0, bytes_accessed=4 * blocks.size, transcendentals=0),
        compiler_params=pltpu.CompilerParams(vmem_limit_bytes=16 * 2**20),
    )(blocks)


def local(tokens, tangent, projector, first_moment, second_moment):
    r = projector.shape[1]
    z, core = lax.axis_index("zh"), lax.axis_index("c")
    tt = turn(tangent)
    half = projector.shape[0] // 2
    share = lax.dynamic_slice_in_dim(projector, core * half, half, 0)
    one, three = back(share, "zh", 4, 1), back(share, "zh", 4, 3)
    part = jnp.dot(tokens, projector, preferred_element_type=F32).astype(BF16)
    part = scattered_sum(part, "x", 4).astype(BF16)
    one, three, tt, share, part = lax.optimization_barrier((one, three, tt, share, part))
    two = back(share, "zh", 4, 2)
    part = scattered_sum(part, "zh", 4).astype(BF16)
    one, two, three, part = lax.optimization_barrier((one, two, three, part))
    mine = jnp.stack([one, two, three])
    other = lax.ppermute(mine, "c", [(0, 1), (1, 0)])
    part = spread(part, "zh", 4).reshape(-1, r)
    at = jnp.stack([z, core]).astype(jnp.int32)
    at, mine, other, part = lax.optimization_barrier((at, mine, other, part))
    reduced = spread(part, "x", 4).reshape(-1, r)
    grad = product(tt, reduced)
    grad = scattered_sum(grad, "c", 2).astype(BF16)
    gradient = scattered_sum(grad, ("y", "zl"), 16)

    new_first = 0.9 * first_moment + 0.1 * gradient
    new_second = 0.999 * second_moment + 0.001 * gradient * gradient
    first_fix = 1.0 - 0.9**STEP
    second_fix = 1.0 - 0.999**STEP
    direction = (new_first / first_fix / (jnp.sqrt(new_second / second_fix) + 1e-08)).astype(BF16)
    rows = direction.shape[0]
    directions = spread(direction, "x", 4).reshape(-1, r)
    out = update_rows(at, directions, projector, mine, other)
    out = lay(swap(out.reshape(4, rows, -1), "x"))
    return (out, new_first, new_second)


def solution(mesh):
    fine = Mesh(mesh.devices.reshape(4, 4, 8, 2, 2), ("zh", "x", "y", "zl", "c"))
    dp, fsdp = ("zh", "x"), ("y", "zl", "c")
    rows = P(dp + fsdp, None)
    return jax.shard_map(
        local,
        mesh=fine,
        in_specs=(P(fsdp, dp), P(fsdp, dp), P(dp, None), rows, rows),
        out_specs=(rows, rows, rows),
        check_vma=False,
    )
```

```python
import jax
import jax.numpy as jnp
from jax import lax
from jax.experimental import pallas as pl
from jax.experimental.pallas import tpu as pltpu
from jax.sharding import Mesh, PartitionSpec as P

STEP = 10
F32 = jnp.float32
BF16 = jnp.bfloat16


def swap(parts, axis):
    return lax.all_to_all(parts, axis, 0, 0)


def add(parts):
    total = parts[0].astype(F32)
    for i in range(1, parts.shape[0]):
        total = total + parts[i].astype(F32)
    return total


def scattered_sum(part, axis, n):
    return add(swap(part.reshape((n, -1) + part.shape[1:]), axis))


def spread(block, axis, n):
    return swap(jnp.broadcast_to(block[None], (n,) + block.shape), axis)


def turn_kernel(in_ref, out_ref):
    turned = in_ref[...].T
    rows = out_ref.shape[2]
    for i in range(out_ref.shape[1]):
        for c in range(2):
            at = (2 * i + c) * rows
            out_ref[c, i] = turned[at : at + rows]


def turn(tangent):
    tokens, hidden = tangent.shape
    rows = hidden // 32
    step = 128 // (2 * rows)
    out = pl.pallas_call(
        turn_kernel,
        grid=(hidden // 128,),
        in_specs=[pl.BlockSpec((tokens, 128), lambda i: (0, i))],
        out_specs=pl.BlockSpec((2, step, rows, tokens), lambda i: (0, i, 0, 0)),
        out_shape=jax.ShapeDtypeStruct((2, 16, rows, tokens), tangent.dtype),
        cost_estimate=pl.CostEstimate(flops=0, bytes_accessed=4 * tokens * hidden, transcendentals=0),
        compiler_params=pltpu.CompilerParams(vmem_limit_bytes=16 * 2**20),
    )(tangent)
    return out.reshape(hidden, tokens)


def product_kernel(a_ref, b_ref, out_ref):
    step = 256

    @pl.loop(0, a_ref.shape[0] // step)
    def _(i):
        at = pl.ds(pl.multiple_of(i * step, step), step)
        out_ref[at] = jnp.dot(a_ref[at], b_ref[...], preferred_element_type=F32).astype(BF16)


def cost(m, k, n):
    return pl.CostEstimate(
        flops=2 * m * k * n, bytes_accessed=2 * (m * k + k * n + m * n), transcendentals=0
    )


def product(a, b):
    vmem = pl.BlockSpec(memory_space=pltpu.VMEM)
    m, k, n = a.shape[0], a.shape[1], b.shape[1]
    return pl.pallas_call(
        product_kernel,
        in_specs=[vmem, vmem],
        out_specs=vmem,
        out_shape=jax.ShapeDtypeStruct((m, n), BF16),
        cost_estimate=cost(m, k, n),
        compiler_params=pltpu.CompilerParams(vmem_limit_bytes=16 * 2**20),
    )(a, b)


def first_kernel(a_ref, b_ref, out_ref):
    out_ref[...] = jnp.dot(a_ref[...], b_ref[...], preferred_element_type=F32).astype(BF16)


def first_product(a, b):
    m, k, n = a.shape[0], a.shape[1], b.shape[1]
    return pl.pallas_call(
        first_kernel,
        grid=(4,),
        in_specs=[
            pl.BlockSpec((m // 4, k), lambda i: (i, 0)),
            pl.BlockSpec((k, n), lambda i: (0, 0)),
        ],
        out_specs=pl.BlockSpec((m // 4, n), lambda i: (i, 0)),
        out_shape=jax.ShapeDtypeStruct((m, n), BF16),
        cost_estimate=cost(m, k, n),
        compiler_params=pltpu.CompilerParams(vmem_limit_bytes=60 * 2**20),
    )(a, b)


def rows_kernel(at_ref, dir_ref, own_ref, far_ref, out_ref):
    own = at_ref[0]
    width = own_ref.shape[0]
    for ref, at in ((own_ref, own), (far_ref, 1 - own)):
        out_ref[:, pl.ds(pl.multiple_of(at * width, width), width)] = lax.dot_general(
            dir_ref[...], ref[...], (((1,), (1,)), ((), ())), preferred_element_type=F32
        ).astype(BF16)


def update_rows(at, directions, own, far):
    m, k = directions.shape
    n = 2 * own.shape[0]
    vmem = pl.BlockSpec(memory_space=pltpu.VMEM)
    return pl.pallas_call(
        rows_kernel,
        in_specs=[pl.BlockSpec(memory_space=pltpu.SMEM)] + [vmem] * 3,
        out_specs=vmem,
        out_shape=jax.ShapeDtypeStruct((m, n), BF16),
        cost_estimate=cost(m, k, n),
        compiler_params=pltpu.CompilerParams(vmem_limit_bytes=16 * 2**20),
    )(at, directions, own, far)


def lay_kernel(in_ref, out_ref):
    n, _, columns = in_ref.shape
    width = columns // 2
    for half in range(2):
        for i in range(n):
            at = (half * n + i) * width
            out_ref[:, at : at + width] = in_ref[i, :, half * width : (half + 1) * width]


def lay(blocks):
    n, rows, columns = blocks.shape
    vmem = pl.BlockSpec(memory_space=pltpu.VMEM)
    return pl.pallas_call(
        lay_kernel,
        in_specs=[vmem],
        out_specs=vmem,
        out_shape=jax.ShapeDtypeStruct((rows, n * columns), blocks.dtype),
        cost_estimate=pl.CostEstimate(flops=0, bytes_accessed=4 * blocks.size, transcendentals=0),
        compiler_params=pltpu.CompilerParams(vmem_limit_bytes=16 * 2**20),
    )(blocks)


def local(tokens, tangent, projector, first_moment, second_moment):
    r = projector.shape[1]
    z = ("za", "zb")
    at = lax.axis_index("za").reshape(1).astype(jnp.int32)
    tt = turn(tangent)
    far = lax.ppermute(projector, "za", [(0, 1), (1, 0)])
    part = first_product(tokens, projector)
    part = scattered_sum(part, "x", 4).astype(BF16)
    at, far, tt, part = lax.optimization_barrier((at, far, tt, part))
    part = scattered_sum(part, z, 4).astype(BF16)
    part = spread(part, z, 4).reshape(-1, r)
    reduced = spread(part, "x", 4).reshape(-1, r)
    grad = product(tt, reduced)
    grad = scattered_sum(grad, "c", 2).astype(BF16)
    gradient = scattered_sum(grad, ("y", "zl"), 16)

    new_first = 0.9 * first_moment + 0.1 * gradient
    new_second = 0.999 * second_moment + 0.001 * gradient * gradient
    first_fix = 1.0 - 0.9**STEP
    second_fix = 1.0 - 0.999**STEP
    direction = (new_first / first_fix / (jnp.sqrt(new_second / second_fix) + 1e-08)).astype(BF16)
    rows = direction.shape[0]
    directions = spread(direction, ("zb", "x"), 8).reshape(-1, r)
    out = update_rows(at, directions, projector, far)
    out = lay(swap(out.reshape(8, rows, -1), ("zb", "x")))
    return (out, new_first, new_second)


def solution(mesh):
    fine = Mesh(mesh.devices.reshape(2, 2, 4, 8, 2, 2), ("za", "zb", "x", "y", "zl", "c"))
    dp, fsdp = ("za", "zb", "x"), ("y", "zl", "c")
    rows = P(dp + fsdp, None)
    return jax.shard_map(
        local,
        mesh=fine,
        in_specs=(P(fsdp, dp), P(fsdp, dp), P(dp, None), rows, rows),
        out_specs=(rows, rows, rows),
        check_vma=False,
    )
```

```python
import jax
import jax.numpy as jnp
from jax import lax
from jax.experimental import pallas as pl
from jax.experimental.pallas import tpu as pltpu
from jax.sharding import Mesh, PartitionSpec as P

STEP = 10
F32 = jnp.float32
BF16 = jnp.bfloat16


def swap(parts, axis):
    return lax.all_to_all(parts, axis, 0, 0)


def add(parts):
    total = parts[0].astype(F32)
    for i in range(1, parts.shape[0]):
        total = total + parts[i].astype(F32)
    return total


def scattered_sum(part, axis, n):
    return add(swap(part.reshape((n, -1) + part.shape[1:]), axis))


def spread(block, axis, n):
    return swap(jnp.broadcast_to(block[None], (n,) + block.shape), axis)


def back(block, axis, n, k):
    return lax.ppermute(block, axis, [(i, (i + k) % n) for i in range(n)])


def turn_kernel(in_ref, out_ref):
    turned = in_ref[...].T
    rows = out_ref.shape[2]
    for i in range(out_ref.shape[1]):
        for c in range(2):
            at = (2 * i + c) * rows
            out_ref[c, i] = turned[at : at + rows]


def turn(tangent):
    tokens, hidden = tangent.shape
    rows = hidden // 32
    step = 128 // (2 * rows)
    out = pl.pallas_call(
        turn_kernel,
        grid=(hidden // 128,),
        in_specs=[pl.BlockSpec((tokens, 128), lambda i: (0, i))],
        out_specs=pl.BlockSpec((2, step, rows, tokens), lambda i: (0, i, 0, 0)),
        out_shape=jax.ShapeDtypeStruct((2, 16, rows, tokens), tangent.dtype),
        cost_estimate=pl.CostEstimate(flops=0, bytes_accessed=4 * tokens * hidden, transcendentals=0),
        compiler_params=pltpu.CompilerParams(vmem_limit_bytes=16 * 2**20),
    )(tangent)
    return out.reshape(hidden, tokens)


def product_kernel(a_ref, b_ref, out_ref):
    step = 256

    @pl.loop(0, a_ref.shape[0] // step)
    def _(i):
        at = pl.ds(pl.multiple_of(i * step, step), step)
        out_ref[at] = jnp.dot(a_ref[at], b_ref[...], preferred_element_type=F32).astype(BF16)


def cost(m, k, n):
    return pl.CostEstimate(
        flops=2 * m * k * n, bytes_accessed=2 * (m * k + k * n + m * n), transcendentals=0
    )


def product(a, b):
    vmem = pl.BlockSpec(memory_space=pltpu.VMEM)
    m, k, n = a.shape[0], a.shape[1], b.shape[1]
    return pl.pallas_call(
        product_kernel,
        in_specs=[vmem, vmem],
        out_specs=vmem,
        out_shape=jax.ShapeDtypeStruct((m, n), BF16),
        cost_estimate=cost(m, k, n),
        compiler_params=pltpu.CompilerParams(vmem_limit_bytes=16 * 2**20),
    )(a, b)


def rows_kernel(z_ref, dir_ref, *refs):
    out_ref = refs[-1]
    width = refs[0].shape[0]
    for k, ref in enumerate(refs[:-1]):
        at = lax.rem(z_ref[0] + 4 - k, 4) * width
        out_ref[:, pl.ds(pl.multiple_of(at, width), width)] = lax.dot_general(
            dir_ref[...], ref[...], (((1,), (1,)), ((), ())), preferred_element_type=F32
        ).astype(BF16)


def update_rows(z, directions, shares):
    m, k = directions.shape
    n = 4 * shares[0].shape[0]
    vmem = pl.BlockSpec(memory_space=pltpu.VMEM)
    return pl.pallas_call(
        rows_kernel,
        in_specs=[pl.BlockSpec(memory_space=pltpu.SMEM)] + [vmem] * 5,
        out_specs=vmem,
        out_shape=jax.ShapeDtypeStruct((m, n), BF16),
        cost_estimate=cost(m, k, n),
        compiler_params=pltpu.CompilerParams(vmem_limit_bytes=16 * 2**20),
    )(z, directions, *shares)


def lay_kernel(in_ref, out_ref):
    n, _, columns = in_ref.shape
    width = columns // 4
    for z in range(4):
        for i in range(n):
            at = (z * n + i) * width
            out_ref[:, at : at + width] = in_ref[i, :, z * width : (z + 1) * width]


def lay(blocks):
    n, rows, columns = blocks.shape
    vmem = pl.BlockSpec(memory_space=pltpu.VMEM)
    return pl.pallas_call(
        lay_kernel,
        in_specs=[vmem],
        out_specs=vmem,
        out_shape=jax.ShapeDtypeStruct((rows, n * columns), blocks.dtype),
        cost_estimate=pl.CostEstimate(flops=0, bytes_accessed=4 * blocks.size, transcendentals=0),
        compiler_params=pltpu.CompilerParams(vmem_limit_bytes=16 * 2**20),
    )(blocks)


def local(tokens, tangent, projector, first_moment, second_moment):
    r = projector.shape[1]
    z = lax.axis_index("zh").reshape(1).astype(jnp.int32)
    tt = turn(tangent)
    half = projector.shape[0] // 2
    share = lax.dynamic_slice_in_dim(projector, lax.axis_index("c") * half, half, 0)
    one, three = back(share, "zh", 4, 1), back(share, "zh", 4, 3)
    part = jnp.dot(tokens, projector, preferred_element_type=F32).astype(BF16)
    part = scattered_sum(part, "x", 4).astype(BF16)
    z, one, three, tt, share, part = lax.optimization_barrier((z, one, three, tt, share, part))
    part = scattered_sum(part, "zh", 4).astype(BF16)
    part = spread(part, "zh", 4).reshape(-1, r)
    reduced = spread(part, "x", 4).reshape(-1, r)
    grad = product(tt, reduced)
    grad = scattered_sum(grad, "c", 2).astype(BF16)
    share, grad = lax.optimization_barrier((share, grad))
    two = back(share, "zh", 4, 2)
    gradient = scattered_sum(grad, ("y", "zl"), 16)
    two, gradient = lax.optimization_barrier((two, gradient))

    new_first = 0.9 * first_moment + 0.1 * gradient
    new_second = 0.999 * second_moment + 0.001 * gradient * gradient
    first_fix = 1.0 - 0.9**STEP
    second_fix = 1.0 - 0.999**STEP
    direction = (new_first / first_fix / (jnp.sqrt(new_second / second_fix) + 1e-08)).astype(BF16)
    rows = direction.shape[0]
    directions = spread(direction, ("x", "c"), 8).reshape(-1, r)
    out = update_rows(z, directions, (share, one, two, three))
    out = lay(swap(out.reshape(8, rows, -1), ("x", "c")))
    return (out, new_first, new_second)


def solution(mesh):
    fine = Mesh(mesh.devices.reshape(4, 4, 8, 2, 2), ("zh", "x", "y", "zl", "c"))
    dp, fsdp = ("zh", "x"), ("y", "zl", "c")
    rows = P(dp + fsdp, None)
    return jax.shard_map(
        local,
        mesh=fine,
        in_specs=(P(fsdp, dp), P(fsdp, dp), P(dp, None), rows, rows),
        out_specs=(rows, rows, rows),
        check_vma=False,
    )
```

```python
import jax
import jax.numpy as jnp
from jax import lax
from jax.experimental import pallas as pl
from jax.experimental.pallas import tpu as pltpu
from jax.sharding import Mesh, PartitionSpec as P

STEP = 10
F32 = jnp.float32
BF16 = jnp.bfloat16


def swap(parts, axis):
    return lax.all_to_all(parts, axis, 0, 0)


def add(parts):
    total = parts[0].astype(F32)
    for i in range(1, parts.shape[0]):
        total = total + parts[i].astype(F32)
    return total


def scattered_sum(part, axis, n):
    return add(swap(part.reshape((n, -1) + part.shape[1:]), axis))


def spread(block, axis, n):
    return swap(jnp.broadcast_to(block[None], (n,) + block.shape), axis)


def back(block, axis, n, k):
    return lax.ppermute(block, axis, [(i, (i + k) % n) for i in range(n)])


def turn_kernel(in_ref, out_ref):
    turned = in_ref[...].T
    rows = out_ref.shape[2]
    for i in range(out_ref.shape[1]):
        for c in range(2):
            at = (2 * i + c) * rows
            out_ref[c, i] = turned[at : at + rows]


def turn(tangent):
    tokens, hidden = tangent.shape
    rows = hidden // 32
    step = 128 // (2 * rows)
    out = pl.pallas_call(
        turn_kernel,
        grid=(hidden // 128,),
        in_specs=[pl.BlockSpec((tokens, 128), lambda i: (0, i))],
        out_specs=pl.BlockSpec((2, step, rows, tokens), lambda i: (0, i, 0, 0)),
        out_shape=jax.ShapeDtypeStruct((2, 16, rows, tokens), tangent.dtype),
        cost_estimate=pl.CostEstimate(flops=0, bytes_accessed=4 * tokens * hidden, transcendentals=0),
        compiler_params=pltpu.CompilerParams(vmem_limit_bytes=16 * 2**20),
    )(tangent)
    return out.reshape(hidden, tokens)


def product_kernel(a_ref, b_ref, out_ref):
    step = 256

    @pl.loop(0, a_ref.shape[0] // step)
    def _(i):
        at = pl.ds(pl.multiple_of(i * step, step), step)
        out_ref[at] = jnp.dot(a_ref[at], b_ref[...], preferred_element_type=F32).astype(BF16)


def cost(m, k, n):
    return pl.CostEstimate(
        flops=2 * m * k * n, bytes_accessed=2 * (m * k + k * n + m * n), transcendentals=0
    )


def product(a, b):
    vmem = pl.BlockSpec(memory_space=pltpu.VMEM)
    m, k, n = a.shape[0], a.shape[1], b.shape[1]
    return pl.pallas_call(
        product_kernel,
        in_specs=[vmem, vmem],
        out_specs=vmem,
        out_shape=jax.ShapeDtypeStruct((m, n), BF16),
        cost_estimate=cost(m, k, n),
        compiler_params=pltpu.CompilerParams(vmem_limit_bytes=16 * 2**20),
    )(a, b)


def rows_kernel(z_ref, dir_ref, *refs):
    out_ref = refs[-1]
    width = refs[0].shape[0]
    for k, ref in enumerate(refs[:-1]):
        at = lax.rem(z_ref[0] + 4 - k, 4) * width
        out_ref[:, pl.ds(pl.multiple_of(at, width), width)] = lax.dot_general(
            dir_ref[...], ref[...], (((1,), (1,)), ((), ())), preferred_element_type=F32
        ).astype(BF16)


def update_rows(z, directions, shares):
    m, k = directions.shape
    n = 4 * shares[0].shape[0]
    vmem = pl.BlockSpec(memory_space=pltpu.VMEM)
    return pl.pallas_call(
        rows_kernel,
        in_specs=[pl.BlockSpec(memory_space=pltpu.SMEM)] + [vmem] * 5,
        out_specs=vmem,
        out_shape=jax.ShapeDtypeStruct((m, n), BF16),
        cost_estimate=cost(m, k, n),
        compiler_params=pltpu.CompilerParams(vmem_limit_bytes=16 * 2**20),
    )(z, directions, *shares)


def lay_kernel(in_ref, out_ref):
    n, _, columns = in_ref.shape
    width = columns // 4
    for z in range(4):
        for i in range(n):
            at = (z * n + i) * width
            out_ref[:, at : at + width] = in_ref[i, :, z * width : (z + 1) * width]


def lay(blocks):
    n, rows, columns = blocks.shape
    vmem = pl.BlockSpec(memory_space=pltpu.VMEM)
    return pl.pallas_call(
        lay_kernel,
        in_specs=[vmem],
        out_specs=vmem,
        out_shape=jax.ShapeDtypeStruct((rows, n * columns), blocks.dtype),
        cost_estimate=pl.CostEstimate(flops=0, bytes_accessed=4 * blocks.size, transcendentals=0),
        compiler_params=pltpu.CompilerParams(vmem_limit_bytes=16 * 2**20),
    )(blocks)


def local(tokens, tangent, projector, first_moment, second_moment):
    r = projector.shape[1]
    z = lax.axis_index("zh").reshape(1).astype(jnp.int32)
    tt = turn(tangent)
    half = projector.shape[0] // 2
    share = lax.dynamic_slice_in_dim(projector, lax.axis_index("c") * half, half, 0)
    one, three = back(share, "zh", 4, 1), back(share, "zh", 4, 3)
    part = jnp.dot(tokens, projector, preferred_element_type=F32).astype(BF16)
    part = scattered_sum(part, "x", 4).astype(BF16)
    z, one, three, tt, share, part = lax.optimization_barrier((z, one, three, tt, share, part))
    part = scattered_sum(part, "zh", 4).astype(BF16)
    part = spread(part, "zh", 4).reshape(-1, r)
    reduced = spread(part, "x", 4).reshape(-1, r)
    grad = product(tt, reduced)
    grad = scattered_sum(grad, "c", 2).astype(BF16)
    one, grad = lax.optimization_barrier((one, grad))
    two = back(one, "zh", 4, 1)
    gradient = scattered_sum(grad, ("y", "zl"), 16)

    new_first = 0.9 * first_moment + 0.1 * gradient
    new_second = 0.999 * second_moment + 0.001 * gradient * gradient
    first_fix = 1.0 - 0.9**STEP
    second_fix = 1.0 - 0.999**STEP
    direction = (new_first / first_fix / (jnp.sqrt(new_second / second_fix) + 1e-08)).astype(BF16)
    rows = direction.shape[0]
    directions = spread(direction, ("x", "c"), 8).reshape(-1, r)
    two, directions = lax.optimization_barrier((two, directions))
    out = update_rows(z, directions, (share, one, two, three))
    out = lay(swap(out.reshape(8, rows, -1), ("x", "c")))
    return (out, new_first, new_second)


def solution(mesh):
    fine = Mesh(mesh.devices.reshape(4, 4, 8, 2, 2), ("zh", "x", "y", "zl", "c"))
    dp, fsdp = ("zh", "x"), ("y", "zl", "c")
    rows = P(dp + fsdp, None)
    return jax.shard_map(
        local,
        mesh=fine,
        in_specs=(P(fsdp, dp), P(fsdp, dp), P(dp, None), rows, rows),
        out_specs=(rows, rows, rows),
        check_vma=False,
    )
```

```python
import functools

import jax
import jax.numpy as jnp
from jax import lax
from jax.experimental import pallas as pl
from jax.experimental.pallas import tpu as pltpu
from jax.sharding import Mesh, PartitionSpec as P

STEP = 10
F32 = jnp.float32
BF16 = jnp.bfloat16


def swap(parts, axis):
    return lax.all_to_all(parts, axis, 0, 0)


def add(parts):
    total = parts[0].astype(F32)
    for i in range(1, parts.shape[0]):
        total = total + parts[i].astype(F32)
    return total


def scattered_sum(part, axis, n):
    return add(swap(part.reshape((n, -1) + part.shape[1:]), axis))


def spread(block, axis, n):
    return swap(jnp.broadcast_to(block[None], (n,) + block.shape), axis)


def back(block, axis, n, k):
    return lax.ppermute(block, axis, [(i, (i + k) % n) for i in range(n)])


def turn_kernel(core_ref, in_ref, out_ref):
    turned = in_ref[...].T
    rows = out_ref.shape[2]
    for i in range(out_ref.shape[1]):
        for c in range(2):
            at = (2 * i + c) * rows
            out_ref[lax.rem(c + core_ref[0], 2), i] = turned[at : at + rows]


def turn(core, tangent):
    tokens, hidden = tangent.shape
    rows = hidden // 32
    step = 128 // (2 * rows)
    out = pl.pallas_call(
        turn_kernel,
        grid=(hidden // 128,),
        in_specs=[
            pl.BlockSpec(memory_space=pltpu.SMEM),
            pl.BlockSpec((tokens, 128), lambda i: (0, i)),
        ],
        out_specs=pl.BlockSpec((2, step, rows, tokens), lambda i: (0, i, 0, 0)),
        out_shape=jax.ShapeDtypeStruct((2, 16, rows, tokens), tangent.dtype),
        cost_estimate=pl.CostEstimate(flops=0, bytes_accessed=4 * tokens * hidden, transcendentals=0),
        compiler_params=pltpu.CompilerParams(vmem_limit_bytes=16 * 2**20),
    )(core, tangent)
    return out.reshape(2, hidden // 2, tokens)


def product_kernel(part, a_ref, b_ref, out_ref):
    step = 256

    @pl.loop(0, a_ref.shape[1] // step)
    def _(i):
        at = pl.ds(pl.multiple_of(i * step, step), step)
        total = jnp.dot(a_ref[part, at], b_ref[...], preferred_element_type=F32)
        out_ref[at] = total.astype(out_ref.dtype)


def cost(m, k, n):
    return pl.CostEstimate(
        flops=2 * m * k * n, bytes_accessed=2 * (m * k + k * n + m * n), transcendentals=0
    )


def product(a, part, b, dtype):
    vmem = pl.BlockSpec(memory_space=pltpu.VMEM)
    m, k, n = a.shape[1], a.shape[2], b.shape[1]
    return pl.pallas_call(
        functools.partial(product_kernel, part),
        in_specs=[vmem, vmem],
        out_specs=vmem,
        out_shape=jax.ShapeDtypeStruct((m, n), dtype),
        cost_estimate=cost(m, k, n),
        compiler_params=pltpu.CompilerParams(vmem_limit_bytes=16 * 2**20),
    )(a, b)


def rows_kernel(z_ref, dir_ref, *refs):
    out_ref = refs[-1]
    width = refs[0].shape[0]
    for k, ref in enumerate(refs[:-1]):
        at = lax.rem(z_ref[0] + 4 - k, 4) * width
        out_ref[:, pl.ds(pl.multiple_of(at, width), width)] = lax.dot_general(
            dir_ref[...], ref[...], (((1,), (1,)), ((), ())), preferred_element_type=F32
        ).astype(BF16)


def update_rows(z, directions, shares):
    m, k = directions.shape
    n = 4 * shares[0].shape[0]
    vmem = pl.BlockSpec(memory_space=pltpu.VMEM)
    return pl.pallas_call(
        rows_kernel,
        in_specs=[pl.BlockSpec(memory_space=pltpu.SMEM)] + [vmem] * 5,
        out_specs=vmem,
        out_shape=jax.ShapeDtypeStruct((m, n), BF16),
        cost_estimate=cost(m, k, n),
        compiler_params=pltpu.CompilerParams(vmem_limit_bytes=16 * 2**20),
    )(z, directions, *shares)


def lay_kernel(in_ref, out_ref):
    n, _, columns = in_ref.shape
    width = columns // 4
    for z in range(4):
        for i in range(n):
            at = (z * n + i) * width
            out_ref[:, at : at + width] = in_ref[i, :, z * width : (z + 1) * width]


def lay(blocks):
    n, rows, columns = blocks.shape
    vmem = pl.BlockSpec(memory_space=pltpu.VMEM)
    return pl.pallas_call(
        lay_kernel,
        in_specs=[vmem],
        out_specs=vmem,
        out_shape=jax.ShapeDtypeStruct((rows, n * columns), blocks.dtype),
        cost_estimate=pl.CostEstimate(flops=0, bytes_accessed=4 * blocks.size, transcendentals=0),
        compiler_params=pltpu.CompilerParams(vmem_limit_bytes=16 * 2**20),
    )(blocks)


def local(tokens, tangent, projector, first_moment, second_moment):
    r = projector.shape[1]
    z = lax.axis_index("zh").reshape(1).astype(jnp.int32)
    core = lax.axis_index("c").reshape(1).astype(jnp.int32)
    tt = turn(core, tangent)
    half = projector.shape[0] // 2
    share = lax.dynamic_slice_in_dim(projector, lax.axis_index("c") * half, half, 0)
    one, three = back(share, "zh", 4, 1), back(share, "zh", 4, 3)
    part = jnp.dot(tokens, projector, preferred_element_type=F32).astype(BF16)
    part = scattered_sum(part, "x", 4).astype(BF16)
    z, one, three, tt, share, part = lax.optimization_barrier((z, one, three, tt, share, part))
    part = scattered_sum(part, "zh", 4).astype(BF16)
    reduced = spread(part, ("x", "zh"), 16).reshape(-1, r)
    others = lax.ppermute(product(tt, 1, reduced, BF16), "c", [(0, 1), (1, 0)])
    grad = (product(tt, 0, reduced, F32) + others.astype(F32)).astype(BF16)
    one, grad = lax.optimization_barrier((one, grad))
    two = back(one, "zh", 4, 1)
    gradient = scattered_sum(grad, ("y", "zl"), 16)

    new_first = 0.9 * first_moment + 0.1 * gradient
    new_second = 0.999 * second_moment + 0.001 * gradient * gradient
    first_fix = 1.0 - 0.9**STEP
    second_fix = 1.0 - 0.999**STEP
    direction = (new_first / first_fix / (jnp.sqrt(new_second / second_fix) + 1e-08)).astype(BF16)
    rows = direction.shape[0]
    directions = spread(direction, ("x", "c"), 8).reshape(-1, r)
    two, directions = lax.optimization_barrier((two, directions))
    out = update_rows(z, directions, (share, one, two, three))
    out = lay(swap(out.reshape(8, rows, -1), ("x", "c")))
    return (out, new_first, new_second)


def solution(mesh):
    fine = Mesh(mesh.devices.reshape(4, 4, 8, 2, 2), ("zh", "x", "y", "zl", "c"))
    dp, fsdp = ("zh", "x"), ("y", "zl", "c")
    rows = P(dp + fsdp, None)
    return jax.shard_map(
        local,
        mesh=fine,
        in_specs=(P(fsdp, dp), P(fsdp, dp), P(dp, None), rows, rows),
        out_specs=(rows, rows, rows),
        check_vma=False,
    )
```

```python
import functools

import jax
import jax.numpy as jnp
from jax import lax
from jax.experimental import pallas as pl
from jax.experimental.pallas import tpu as pltpu
from jax.sharding import Mesh, PartitionSpec as P

STEP = 10
F32 = jnp.float32
BF16 = jnp.bfloat16


def swap(parts, axis):
    return lax.all_to_all(parts, axis, 0, 0)


def add(parts):
    total = parts[0].astype(F32)
    for i in range(1, parts.shape[0]):
        total = total + parts[i].astype(F32)
    return total


def scattered_sum(part, axis, n):
    return add(swap(part.reshape((n, -1) + part.shape[1:]), axis))


def spread(block, axis, n):
    return swap(jnp.broadcast_to(block[None], (n,) + block.shape), axis)


def back(block, axis, n, k):
    return lax.ppermute(block, axis, [(i, (i + k) % n) for i in range(n)])


def turn_kernel(core_ref, in_ref, out_ref):
    turned = in_ref[...].T
    rows = out_ref.shape[2]
    for i in range(out_ref.shape[1]):
        for c in range(2):
            at = (2 * i + c) * rows
            out_ref[lax.rem(c + core_ref[0], 2), i] = turned[at : at + rows]


def turn(core, tangent):
    tokens, hidden = tangent.shape
    rows = hidden // 32
    step = 128 // (2 * rows)
    out = pl.pallas_call(
        turn_kernel,
        grid=(hidden // 128,),
        in_specs=[
            pl.BlockSpec(memory_space=pltpu.SMEM),
            pl.BlockSpec((tokens, 128), lambda i: (0, i)),
        ],
        out_specs=pl.BlockSpec((2, step, rows, tokens), lambda i: (0, i, 0, 0)),
        out_shape=jax.ShapeDtypeStruct((2, 16, rows, tokens), tangent.dtype),
        cost_estimate=pl.CostEstimate(flops=0, bytes_accessed=4 * tokens * hidden, transcendentals=0),
        compiler_params=pltpu.CompilerParams(vmem_limit_bytes=16 * 2**20),
    )(core, tangent)
    return out.reshape(2, hidden // 2, tokens)


def product_kernel(part, a_ref, b_ref, out_ref):
    step = 256

    @pl.loop(0, a_ref.shape[1] // step)
    def _(i):
        at = pl.ds(pl.multiple_of(i * step, step), step)
        total = jnp.dot(a_ref[part, at], b_ref[...], preferred_element_type=F32)
        out_ref[at] = total.astype(out_ref.dtype)


def cost(m, k, n):
    return pl.CostEstimate(
        flops=2 * m * k * n, bytes_accessed=2 * (m * k + k * n + m * n), transcendentals=0
    )


def product(a, part, b, dtype):
    vmem = pl.BlockSpec(memory_space=pltpu.VMEM)
    m, k, n = a.shape[1], a.shape[2], b.shape[1]
    return pl.pallas_call(
        functools.partial(product_kernel, part),
        in_specs=[vmem, vmem],
        out_specs=vmem,
        out_shape=jax.ShapeDtypeStruct((m, n), dtype),
        cost_estimate=cost(m, k, n),
        compiler_params=pltpu.CompilerParams(vmem_limit_bytes=16 * 2**20),
    )(a, b)


def rows_kernel(z_ref, dir_ref, *refs):
    out_ref = refs[-1]
    width = refs[0].shape[0]
    for k, ref in enumerate(refs[:-1]):
        at = lax.rem(z_ref[0] + 4 - k, 4) * width
        out_ref[:, pl.ds(pl.multiple_of(at, width), width)] = lax.dot_general(
            dir_ref[...], ref[...], (((1,), (1,)), ((), ())), preferred_element_type=F32
        ).astype(BF16)


def update_rows(z, directions, shares):
    m, k = directions.shape
    n = 4 * shares[0].shape[0]
    vmem = pl.BlockSpec(memory_space=pltpu.VMEM)
    return pl.pallas_call(
        rows_kernel,
        in_specs=[pl.BlockSpec(memory_space=pltpu.SMEM)] + [vmem] * 5,
        out_specs=vmem,
        out_shape=jax.ShapeDtypeStruct((m, n), BF16),
        cost_estimate=cost(m, k, n),
        compiler_params=pltpu.CompilerParams(vmem_limit_bytes=16 * 2**20),
    )(z, directions, *shares)


def lay_kernel(in_ref, out_ref):
    n, _, columns = in_ref.shape
    width = columns // 4
    for z in range(4):
        for i in range(n):
            at = (z * n + i) * width
            out_ref[:, at : at + width] = in_ref[i, :, z * width : (z + 1) * width]


def lay(blocks):
    n, rows, columns = blocks.shape
    vmem = pl.BlockSpec(memory_space=pltpu.VMEM)
    return pl.pallas_call(
        lay_kernel,
        in_specs=[vmem],
        out_specs=vmem,
        out_shape=jax.ShapeDtypeStruct((rows, n * columns), blocks.dtype),
        cost_estimate=pl.CostEstimate(flops=0, bytes_accessed=4 * blocks.size, transcendentals=0),
        compiler_params=pltpu.CompilerParams(vmem_limit_bytes=16 * 2**20),
    )(blocks)


def local(tokens, tangent, projector, first_moment, second_moment):
    r = projector.shape[1]
    z = lax.axis_index("zh").reshape(1).astype(jnp.int32)
    core = lax.axis_index("c").reshape(1).astype(jnp.int32)
    tt = turn(core, tangent)
    half = projector.shape[0] // 2
    share = lax.dynamic_slice_in_dim(projector, lax.axis_index("c") * half, half, 0)
    one = back(share, "zh", 4, 1)
    part = jnp.dot(tokens, projector, preferred_element_type=F32).astype(BF16)
    part = scattered_sum(part, "x", 4).astype(BF16)
    z, one, tt, share, part = lax.optimization_barrier((z, one, tt, share, part))
    part = scattered_sum(part, "zh", 4).astype(BF16)
    part = spread(part, "zh", 4).reshape(-1, r)
    reduced = spread(part, "x", 4).reshape(-1, r)
    others = lax.ppermute(product(tt, 1, reduced, BF16), "c", [(0, 1), (1, 0)])
    grad = (product(tt, 0, reduced, F32) + others.astype(F32)).astype(BF16)
    one, share, grad = lax.optimization_barrier((one, share, grad))
    two, three = back(one, "zh", 4, 1), back(share, "zh", 4, 3)
    gradient = scattered_sum(grad, ("y", "zl"), 16)

    new_first = 0.9 * first_moment + 0.1 * gradient
    new_second = 0.999 * second_moment + 0.001 * gradient * gradient
    first_fix = 1.0 - 0.9**STEP
    second_fix = 1.0 - 0.999**STEP
    direction = (new_first / first_fix / (jnp.sqrt(new_second / second_fix) + 1e-08)).astype(BF16)
    rows = direction.shape[0]
    directions = spread(direction, ("x", "c"), 8).reshape(-1, r)
    two, three, directions = lax.optimization_barrier((two, three, directions))
    out = update_rows(z, directions, (share, one, two, three))
    out = lay(swap(out.reshape(8, rows, -1), ("x", "c")))
    return (out, new_first, new_second)


def solution(mesh):
    fine = Mesh(mesh.devices.reshape(4, 4, 8, 2, 2), ("zh", "x", "y", "zl", "c"))
    dp, fsdp = ("zh", "x"), ("y", "zl", "c")
    rows = P(dp + fsdp, None)
    return jax.shard_map(
        local,
        mesh=fine,
        in_specs=(P(fsdp, dp), P(fsdp, dp), P(dp, None), rows, rows),
        out_specs=(rows, rows, rows),
        check_vma=False,
    )
```

```python
import functools

import jax
import jax.numpy as jnp
from jax import lax
from jax.experimental import pallas as pl
from jax.experimental.pallas import tpu as pltpu
from jax.sharding import Mesh, PartitionSpec as P

STEP = 10
F32 = jnp.float32
BF16 = jnp.bfloat16


def swap(parts, axis):
    return lax.all_to_all(parts, axis, 0, 0)


def add(parts):
    total = parts[0].astype(F32)
    for i in range(1, parts.shape[0]):
        total = total + parts[i].astype(F32)
    return total


def scattered_sum(part, axis, n):
    return add(swap(part.reshape((n, -1) + part.shape[1:]), axis))


def spread(block, axis, n):
    return swap(jnp.broadcast_to(block[None], (n,) + block.shape), axis)


def back(block, axis, n, k):
    return lax.ppermute(block, axis, [(i, (i + k) % n) for i in range(n)])


def turn_kernel(core_ref, in_ref, out_ref):
    turned = in_ref[...].T
    rows = out_ref.shape[2]
    for i in range(out_ref.shape[1]):
        for c in range(2):
            at = (2 * i + c) * rows
            out_ref[lax.rem(c + core_ref[0], 2), i] = turned[at : at + rows]


def turn(core, tangent):
    tokens, hidden = tangent.shape
    rows = hidden // 32
    step = 128 // (2 * rows)
    out = pl.pallas_call(
        turn_kernel,
        grid=(hidden // 128,),
        in_specs=[
            pl.BlockSpec(memory_space=pltpu.SMEM),
            pl.BlockSpec((tokens, 128), lambda i: (0, i)),
        ],
        out_specs=pl.BlockSpec((2, step, rows, tokens), lambda i: (0, i, 0, 0)),
        out_shape=jax.ShapeDtypeStruct((2, 16, rows, tokens), tangent.dtype),
        cost_estimate=pl.CostEstimate(flops=0, bytes_accessed=4 * tokens * hidden, transcendentals=0),
        compiler_params=pltpu.CompilerParams(vmem_limit_bytes=16 * 2**20),
    )(core, tangent)
    return out.reshape(2, hidden // 2, tokens)


def product_kernel(part, a_ref, b_ref, out_ref):
    step = 256

    @pl.loop(0, a_ref.shape[1] // step)
    def _(i):
        at = pl.ds(pl.multiple_of(i * step, step), step)
        total = jnp.dot(a_ref[part, at], b_ref[...], preferred_element_type=F32)
        out_ref[at] = total.astype(out_ref.dtype)


def cost(m, k, n):
    return pl.CostEstimate(
        flops=2 * m * k * n, bytes_accessed=2 * (m * k + k * n + m * n), transcendentals=0
    )


def product(a, part, b, dtype):
    vmem = pl.BlockSpec(memory_space=pltpu.VMEM)
    m, k, n = a.shape[1], a.shape[2], b.shape[1]
    return pl.pallas_call(
        functools.partial(product_kernel, part),
        in_specs=[vmem, vmem],
        out_specs=vmem,
        out_shape=jax.ShapeDtypeStruct((m, n), dtype),
        cost_estimate=cost(m, k, n),
        compiler_params=pltpu.CompilerParams(vmem_limit_bytes=16 * 2**20),
    )(a, b)


def rows_kernel(z_ref, dir_ref, *refs):
    out_ref = refs[-1]
    width = refs[0].shape[0]
    for k, ref in enumerate(refs[:-1]):
        at = lax.rem(z_ref[0] + 4 - k, 4) * width
        out_ref[:, pl.ds(pl.multiple_of(at, width), width)] = lax.dot_general(
            dir_ref[...], ref[...], (((1,), (1,)), ((), ())), preferred_element_type=F32
        ).astype(BF16)


def update_rows(z, directions, shares):
    m, k = directions.shape
    n = 4 * shares[0].shape[0]
    vmem = pl.BlockSpec(memory_space=pltpu.VMEM)
    return pl.pallas_call(
        rows_kernel,
        in_specs=[pl.BlockSpec(memory_space=pltpu.SMEM)] + [vmem] * 5,
        out_specs=vmem,
        out_shape=jax.ShapeDtypeStruct((m, n), BF16),
        cost_estimate=cost(m, k, n),
        compiler_params=pltpu.CompilerParams(vmem_limit_bytes=16 * 2**20),
    )(z, directions, *shares)


def lay_kernel(in_ref, out_ref):
    n, _, columns = in_ref.shape
    width = columns // 4
    for z in range(4):
        for i in range(n):
            at = (z * n + i) * width
            out_ref[:, at : at + width] = in_ref[i, :, z * width : (z + 1) * width]


def lay(blocks):
    n, rows, columns = blocks.shape
    vmem = pl.BlockSpec(memory_space=pltpu.VMEM)
    return pl.pallas_call(
        lay_kernel,
        in_specs=[vmem],
        out_specs=vmem,
        out_shape=jax.ShapeDtypeStruct((rows, n * columns), blocks.dtype),
        cost_estimate=pl.CostEstimate(flops=0, bytes_accessed=4 * blocks.size, transcendentals=0),
        compiler_params=pltpu.CompilerParams(vmem_limit_bytes=16 * 2**20),
    )(blocks)


def local(tokens, tangent, projector, first_moment, second_moment):
    r = projector.shape[1]
    z = lax.axis_index("zh").reshape(1).astype(jnp.int32)
    core = lax.axis_index("c").reshape(1).astype(jnp.int32)
    tt = turn(core, tangent)
    half = projector.shape[0] // 2
    share = lax.dynamic_slice_in_dim(projector, lax.axis_index("c") * half, half, 0)
    one = back(share, "zh", 4, 1)
    part = jnp.dot(tokens, projector, preferred_element_type=F32).astype(BF16)
    part = scattered_sum(part, "x", 4).astype(BF16)
    z, one, tt, share, part = lax.optimization_barrier((z, one, tt, share, part))
    others = [back(part, "zh", 4, k) for k in (1, 3, 2)]
    part = sum((o.astype(F32) for o in others), part.astype(F32)).astype(BF16)
    reduced = spread(part, "x", 4).reshape(-1, r)
    others = lax.ppermute(product(tt, 1, reduced, BF16), "c", [(0, 1), (1, 0)])
    grad = (product(tt, 0, reduced, F32) + others.astype(F32)).astype(BF16)
    one, share, grad = lax.optimization_barrier((one, share, grad))
    two, three = back(one, "zh", 4, 1), back(share, "zh", 4, 3)
    gradient = scattered_sum(grad, ("y", "zl"), 16)

    new_first = 0.9 * first_moment + 0.1 * gradient
    new_second = 0.999 * second_moment + 0.001 * gradient * gradient
    first_fix = 1.0 - 0.9**STEP
    second_fix = 1.0 - 0.999**STEP
    direction = (new_first / first_fix / (jnp.sqrt(new_second / second_fix) + 1e-08)).astype(BF16)
    rows = direction.shape[0]
    directions = spread(direction, ("x", "c"), 8).reshape(-1, r)
    two, three, directions = lax.optimization_barrier((two, three, directions))
    out = update_rows(z, directions, (share, one, two, three))
    out = lay(swap(out.reshape(8, rows, -1), ("x", "c")))
    return (out, new_first, new_second)


def solution(mesh):
    fine = Mesh(mesh.devices.reshape(4, 4, 8, 2, 2), ("zh", "x", "y", "zl", "c"))
    dp, fsdp = ("zh", "x"), ("y", "zl", "c")
    rows = P(dp + fsdp, None)
    return jax.shard_map(
        local,
        mesh=fine,
        in_specs=(P(fsdp, dp), P(fsdp, dp), P(dp, None), rows, rows),
        out_specs=(rows, rows, rows),
        check_vma=False,
    )
```

```python
import functools

import jax
import jax.numpy as jnp
from jax import lax
from jax.experimental import pallas as pl
from jax.experimental.pallas import tpu as pltpu
from jax.sharding import Mesh, PartitionSpec as P

STEP = 10
F32 = jnp.float32
BF16 = jnp.bfloat16


def swap(parts, axis):
    return lax.all_to_all(parts, axis, 0, 0)


def add(parts):
    total = parts[0].astype(F32)
    for i in range(1, parts.shape[0]):
        total = total + parts[i].astype(F32)
    return total


def scattered_sum(part, axis, n):
    return add(swap(part.reshape((n, -1) + part.shape[1:]), axis))


def spread(block, axis, n):
    return swap(jnp.broadcast_to(block[None], (n,) + block.shape), axis)


def back(block, axis, n, k):
    return lax.ppermute(block, axis, [(i, (i + k) % n) for i in range(n)])


def turn_kernel(core_ref, in_ref, out_ref):
    turned = in_ref[...].T
    rows = out_ref.shape[2]
    for i in range(out_ref.shape[1]):
        for c in range(2):
            at = (2 * i + c) * rows
            out_ref[lax.rem(c + core_ref[0], 2), i] = turned[at : at + rows]


def turn(core, tangent):
    tokens, hidden = tangent.shape
    rows = hidden // 32
    step = 128 // (2 * rows)
    out = pl.pallas_call(
        turn_kernel,
        grid=(hidden // 128,),
        in_specs=[
            pl.BlockSpec(memory_space=pltpu.SMEM),
            pl.BlockSpec((tokens, 128), lambda i: (0, i)),
        ],
        out_specs=pl.BlockSpec((2, step, rows, tokens), lambda i: (0, i, 0, 0)),
        out_shape=jax.ShapeDtypeStruct((2, 16, rows, tokens), tangent.dtype),
        cost_estimate=pl.CostEstimate(flops=0, bytes_accessed=4 * tokens * hidden, transcendentals=0),
        compiler_params=pltpu.CompilerParams(vmem_limit_bytes=16 * 2**20),
    )(core, tangent)
    return out.reshape(2, hidden // 2, tokens)


def product_kernel(part, a_ref, b_ref, out_ref):
    step = 256

    @pl.loop(0, a_ref.shape[1] // step)
    def _(i):
        at = pl.ds(pl.multiple_of(i * step, step), step)
        total = jnp.dot(a_ref[part, at], b_ref[...], preferred_element_type=F32)
        out_ref[at] = total.astype(out_ref.dtype)


def cost(m, k, n):
    return pl.CostEstimate(
        flops=2 * m * k * n, bytes_accessed=2 * (m * k + k * n + m * n), transcendentals=0
    )


def product(a, part, b, dtype):
    vmem = pl.BlockSpec(memory_space=pltpu.VMEM)
    m, k, n = a.shape[1], a.shape[2], b.shape[1]
    return pl.pallas_call(
        functools.partial(product_kernel, part),
        in_specs=[vmem, vmem],
        out_specs=vmem,
        out_shape=jax.ShapeDtypeStruct((m, n), dtype),
        cost_estimate=cost(m, k, n),
        compiler_params=pltpu.CompilerParams(vmem_limit_bytes=16 * 2**20),
    )(a, b)


def rows_kernel(z_ref, dir_ref, *refs):
    out_ref = refs[-1]
    width = refs[0].shape[0]
    for k, ref in enumerate(refs[:-1]):
        at = lax.rem(z_ref[0] + 4 - k, 4) * width
        out_ref[:, pl.ds(pl.multiple_of(at, width), width)] = lax.dot_general(
            dir_ref[...], ref[...], (((1,), (1,)), ((), ())), preferred_element_type=F32
        ).astype(BF16)


def update_rows(z, directions, shares):
    m, k = directions.shape
    n = 4 * shares[0].shape[0]
    vmem = pl.BlockSpec(memory_space=pltpu.VMEM)
    return pl.pallas_call(
        rows_kernel,
        in_specs=[pl.BlockSpec(memory_space=pltpu.SMEM)] + [vmem] * 5,
        out_specs=vmem,
        out_shape=jax.ShapeDtypeStruct((m, n), BF16),
        cost_estimate=cost(m, k, n),
        compiler_params=pltpu.CompilerParams(vmem_limit_bytes=16 * 2**20),
    )(z, directions, *shares)


def lay_kernel(in_ref, out_ref):
    n, _, columns = in_ref.shape
    width = columns // 4
    for z in range(4):
        for i in range(n):
            at = (z * n + i) * width
            out_ref[:, at : at + width] = in_ref[i, :, z * width : (z + 1) * width]


def lay(blocks):
    n, rows, columns = blocks.shape
    vmem = pl.BlockSpec(memory_space=pltpu.VMEM)
    return pl.pallas_call(
        lay_kernel,
        in_specs=[vmem],
        out_specs=vmem,
        out_shape=jax.ShapeDtypeStruct((rows, n * columns), blocks.dtype),
        cost_estimate=pl.CostEstimate(flops=0, bytes_accessed=4 * blocks.size, transcendentals=0),
        compiler_params=pltpu.CompilerParams(vmem_limit_bytes=16 * 2**20),
    )(blocks)


def local(tokens, tangent, projector, first_moment, second_moment):
    r = projector.shape[1]
    z = lax.axis_index("zh").reshape(1).astype(jnp.int32)
    core = lax.axis_index("c").reshape(1).astype(jnp.int32)
    tt = turn(core, tangent)
    half = projector.shape[0] // 2
    share = lax.dynamic_slice_in_dim(projector, lax.axis_index("c") * half, half, 0)
    part = jnp.dot(tokens, projector, preferred_element_type=F32).astype(BF16)
    part = scattered_sum(part, ("x", "zh"), 16).astype(BF16)
    z, tt, share, part = lax.optimization_barrier((z, tt, share, part))
    part = spread(part, "zh", 4).reshape(-1, r)
    reduced = spread(part, "x", 4).reshape(-1, r)
    share, reduced = lax.optimization_barrier((share, reduced))
    one = back(share, "zh", 4, 1)
    others = lax.ppermute(product(tt, 1, reduced, BF16), "c", [(0, 1), (1, 0)])
    grad = (product(tt, 0, reduced, F32) + others.astype(F32)).astype(BF16)
    share, grad = lax.optimization_barrier((share, grad))
    two, three = back(one, "zh", 4, 1), back(share, "zh", 4, 3)
    gradient = scattered_sum(grad, ("y", "zl"), 16)

    new_first = 0.9 * first_moment + 0.1 * gradient
    new_second = 0.999 * second_moment + 0.001 * gradient * gradient
    first_fix = 1.0 - 0.9**STEP
    second_fix = 1.0 - 0.999**STEP
    direction = (new_first / first_fix / (jnp.sqrt(new_second / second_fix) + 1e-08)).astype(BF16)
    rows = direction.shape[0]
    directions = spread(direction, ("x", "c"), 8).reshape(-1, r)
    two, three, directions = lax.optimization_barrier((two, three, directions))
    out = update_rows(z, directions, (share, one, two, three))
    out = lay(swap(out.reshape(8, rows, -1), ("x", "c")))
    return (out, new_first, new_second)


def solution(mesh):
    fine = Mesh(mesh.devices.reshape(4, 4, 8, 2, 2), ("zh", "x", "y", "zl", "c"))
    dp, fsdp = ("zh", "x"), ("y", "zl", "c")
    rows = P(dp + fsdp, None)
    return jax.shard_map(
        local,
        mesh=fine,
        in_specs=(P(fsdp, dp), P(fsdp, dp), P(dp, None), rows, rows),
        out_specs=(rows, rows, rows),
        check_vma=False,
    )
```

```python
import functools

import jax
import jax.numpy as jnp
from jax import lax
from jax.experimental import pallas as pl
from jax.experimental.pallas import tpu as pltpu
from jax.sharding import Mesh, PartitionSpec as P

STEP = 10
F32 = jnp.float32
BF16 = jnp.bfloat16


def swap(parts, axis):
    return lax.all_to_all(parts, axis, 0, 0)


def add(parts):
    total = parts[0].astype(F32)
    for i in range(1, parts.shape[0]):
        total = total + parts[i].astype(F32)
    return total


def scattered_sum(part, axis, n):
    return add(swap(part.reshape((n, -1) + part.shape[1:]), axis))


def spread(block, axis, n):
    return swap(jnp.broadcast_to(block[None], (n,) + block.shape), axis)


def back(block, axis, n, k):
    return lax.ppermute(block, axis, [(i, (i + k) % n) for i in range(n)])


def turn_kernel(core_ref, in_ref, out_ref):
    turned = in_ref[...].T
    rows = out_ref.shape[2]
    for i in range(out_ref.shape[1]):
        for c in range(2):
            at = (2 * i + c) * rows
            out_ref[lax.rem(c + core_ref[0], 2), i] = turned[at : at + rows]


def turn(core, tangent):
    tokens, hidden = tangent.shape
    rows = hidden // 32
    step = 128 // (2 * rows)
    out = pl.pallas_call(
        turn_kernel,
        grid=(hidden // 128,),
        in_specs=[
            pl.BlockSpec(memory_space=pltpu.SMEM),
            pl.BlockSpec((tokens, 128), lambda i: (0, i)),
        ],
        out_specs=pl.BlockSpec((2, step, rows, tokens), lambda i: (0, i, 0, 0)),
        out_shape=jax.ShapeDtypeStruct((2, 16, rows, tokens), tangent.dtype),
        cost_estimate=pl.CostEstimate(flops=0, bytes_accessed=4 * tokens * hidden, transcendentals=0),
        compiler_params=pltpu.CompilerParams(vmem_limit_bytes=16 * 2**20),
    )(core, tangent)
    return out.reshape(2, hidden // 2, tokens)


def product_kernel(part, a_ref, b_ref, out_ref):
    step = 256

    @pl.loop(0, a_ref.shape[1] // step)
    def _(i):
        at = pl.ds(pl.multiple_of(i * step, step), step)
        total = jnp.dot(a_ref[part, at], b_ref[...], preferred_element_type=F32)
        out_ref[at] = total.astype(out_ref.dtype)


def cost(m, k, n):
    return pl.CostEstimate(
        flops=2 * m * k * n, bytes_accessed=2 * (m * k + k * n + m * n), transcendentals=0
    )


def product(a, part, b, dtype):
    vmem = pl.BlockSpec(memory_space=pltpu.VMEM)
    m, k, n = a.shape[1], a.shape[2], b.shape[1]
    return pl.pallas_call(
        functools.partial(product_kernel, part),
        in_specs=[vmem, vmem],
        out_specs=vmem,
        out_shape=jax.ShapeDtypeStruct((m, n), dtype),
        cost_estimate=cost(m, k, n),
        compiler_params=pltpu.CompilerParams(vmem_limit_bytes=16 * 2**20),
    )(a, b)


def rows_kernel(z_ref, dir_ref, *refs):
    out_ref = refs[-1]
    width = refs[0].shape[0]
    for k, ref in enumerate(refs[:-1]):
        at = lax.rem(z_ref[0] + 4 - k, 4) * width
        out_ref[:, pl.ds(pl.multiple_of(at, width), width)] = lax.dot_general(
            dir_ref[...], ref[...], (((1,), (1,)), ((), ())), preferred_element_type=F32
        ).astype(BF16)


def update_rows(z, directions, shares):
    m, k = directions.shape
    n = 4 * shares[0].shape[0]
    vmem = pl.BlockSpec(memory_space=pltpu.VMEM)
    return pl.pallas_call(
        rows_kernel,
        in_specs=[pl.BlockSpec(memory_space=pltpu.SMEM)] + [vmem] * 5,
        out_specs=vmem,
        out_shape=jax.ShapeDtypeStruct((m, n), BF16),
        cost_estimate=cost(m, k, n),
        compiler_params=pltpu.CompilerParams(vmem_limit_bytes=16 * 2**20),
    )(z, directions, *shares)


def lay_kernel(in_ref, out_ref):
    n, _, columns = in_ref.shape
    width = columns // 4
    for z in range(4):
        for i in range(n):
            at = (z * n + i) * width
            out_ref[:, at : at + width] = in_ref[i, :, z * width : (z + 1) * width]


def lay(blocks):
    n, rows, columns = blocks.shape
    vmem = pl.BlockSpec(memory_space=pltpu.VMEM)
    return pl.pallas_call(
        lay_kernel,
        in_specs=[vmem],
        out_specs=vmem,
        out_shape=jax.ShapeDtypeStruct((rows, n * columns), blocks.dtype),
        cost_estimate=pl.CostEstimate(flops=0, bytes_accessed=4 * blocks.size, transcendentals=0),
        compiler_params=pltpu.CompilerParams(vmem_limit_bytes=16 * 2**20),
    )(blocks)


def local(tokens, tangent, projector, first_moment, second_moment):
    r = projector.shape[1]
    z = lax.axis_index("zh").reshape(1).astype(jnp.int32)
    core = lax.axis_index("c").reshape(1).astype(jnp.int32)
    tt = turn(core, tangent)
    half = projector.shape[0] // 2
    share = lax.dynamic_slice_in_dim(projector, lax.axis_index("c") * half, half, 0)
    one = back(share, "zh", 4, 1)
    part = jnp.dot(tokens, projector, preferred_element_type=F32).astype(BF16)
    part = scattered_sum(part, "x", 4).astype(BF16)
    z, one, tt, share, part = lax.optimization_barrier((z, one, tt, share, part))
    part = scattered_sum(part, "zh", 4).astype(BF16)
    part = spread(part, "zh", 4).reshape(-1, r)
    reduced = spread(part, "x", 4).reshape(-1, r)
    others = lax.ppermute(product(tt, 1, reduced, BF16), "c", [(0, 1), (1, 0)])
    grad = (product(tt, 0, reduced, F32) + others.astype(F32)).astype(BF16)
    one, share, grad = lax.optimization_barrier((one, share, grad))
    two, three = back(one, "zh", 4, 1), back(share, "zh", 4, 3)
    gradient = scattered_sum(grad, ("y", "zl"), 16)
    two, three, gradient = lax.optimization_barrier((two, three, gradient))

    new_first = 0.9 * first_moment + 0.1 * gradient
    new_second = 0.999 * second_moment + 0.001 * gradient * gradient
    first_fix = 1.0 - 0.9**STEP
    second_fix = 1.0 - 0.999**STEP
    direction = (new_first / first_fix / (jnp.sqrt(new_second / second_fix) + 1e-08)).astype(BF16)
    rows = direction.shape[0]
    directions = spread(direction, ("x", "c"), 8).reshape(-1, r)
    out = update_rows(z, directions, (share, one, two, three))
    out = lay(swap(out.reshape(8, rows, -1), ("x", "c")))
    return (out, new_first, new_second)


def solution(mesh):
    fine = Mesh(mesh.devices.reshape(4, 4, 8, 2, 2), ("zh", "x", "y", "zl", "c"))
    dp, fsdp = ("zh", "x"), ("y", "zl", "c")
    rows = P(dp + fsdp, None)
    return jax.shard_map(
        local,
        mesh=fine,
        in_specs=(P(fsdp, dp), P(fsdp, dp), P(dp, None), rows, rows),
        out_specs=(rows, rows, rows),
        check_vma=False,
    )
```
